256 devices in a mesh: rep: 4 (over x), ep: 64 (over y, z, core).
Axes of the slice: x: 4, y: 4, z: 8, core: 2. Of those that a mesh axis runs over, the one named last changes fastest.
Arguments:
- tokens: bfloat16 [32768, 4096], P(('rep', 'ep')), may hold values from -6 to 6
- cotangent: bfloat16 [32768, 4096], P(('rep', 'ep')), may hold values from -6 to 6
- expert_ids: int32 [32768, 1], P(('rep', 'ep')), may hold values from 0 to 63; in each aligned block of 128 rows (0 to 127, 128 to 255, ...) at most 4 rows name the same one
- gates: bfloat16 [32768, 1], P(('rep', 'ep')), may hold values from 0.19921875 to 1.5
- gate_weight: bfloat16 [64, 4096, 768], P('ep', None, 'rep'), may hold values from -0.09375 to 0.09375
- up_weight: bfloat16 [64, 4096, 768], P('ep', None, 'rep'), may hold values from -0.09375 to 0.09375
- down_weight: bfloat16 [64, 768, 4096], P('ep', 'rep'), may hold values from -0.21875 to 0.21875
Outputs:
- token_grad: bfloat16 [32768, 4096], P(('rep', 'ep'))
- gates_grad: bfloat16 [32768, 1], P(('rep', 'ep'))
- gate_weight_grad: bfloat16 [64, 4096, 768], P('ep', None, 'rep')
- up_weight_grad: bfloat16 [64, 4096, 768], P('ep', None, 'rep')
- down_weight_grad: bfloat16 [64, 768, 4096], P('ep', 'rep')
The draws below stay inside these ranges and needn't reach their ends.
Inputs may be any that keep to these rules, and one draw needn't show every extreme that they name: `expert_ids`: each token names exactly 1 expert. Within the rows of one device (aligned blocks of 128 tokens) no expert is named by more than 4 rows, a bound that some block reaches.
All inputs are finite; a program needn't handle non-finite values.
Results may differ from the reference program's by a relative error of at most 0.02.
Values may be sent and summed in bfloat16 or wider, within the bound.
A program may use at most 192 MiB of HBM per device.

```python
import math
import jax
import jax.numpy as jnp
import numpy as np
from jax import lax

D = 4096
H = 768
TOPK = 1
TOK_DEV = 128
EXPERTS = 64
TOKENS = 32768
CAP = 4
N_REP = 4
DEVICES = 256


def steps_of(rng, shape, pieces, least, high):
    gain, own = 1.0, jax.random.fold_in(rng, 6)
    for axis_at, parts in pieces:
        steps = jnp.exp(jax.random.uniform(jax.random.fold_in(own, axis_at), (parts,), jnp.float32, least / len(pieces), high / len(pieces)))
        gain = gain * jnp.repeat(steps, shape[axis_at] // parts).reshape([-1 if axis == axis_at else 1 for axis in range(len(shape))])
    return gain


def deal_out(stream_key, own, number, rows, amount, top, most, slope):
    ranking = jax.random.permutation(stream_key, amount)
    heavy_load, ordinary = shares(amount, rows * top, most, slope, True), shares(amount, rows * top, most, slope, False)
    places = jnp.arange(amount)

    def named(lengths, offset_by):
        used = int((lengths > 0).sum())
        fixed = max(1, used // 4)
        passed = fixed + (places - fixed + offset_by * (used - fixed)) % max(1, amount - fixed)
        return jnp.zeros((amount,), jnp.int32).at[ranking[jnp.where(places < fixed, places, passed)]].set(jnp.asarray(lengths, jnp.int32))

    lengths = jnp.where(number % 4 == 0, named(heavy_load, number // 4), named(ordinary, number - number // 4 - 1))
    mixed = jax.random.permutation(jax.random.fold_in(own, 3), amount)
    source_of, receiver = mixed[0:amount // 2 * 2:2], mixed[1:amount // 2 * 2:2]
    room = jnp.minimum(lengths[source_of] - 1, most - lengths[receiver]) // 2
    room = jnp.where((source_of == ranking[0]) | (receiver == ranking[0]) | (lengths[receiver] == 0), 0, jnp.maximum(room, 0))
    passed = jax.random.randint(jax.random.fold_in(own, 4), (amount // 2,), 0, 1 << 20) % (room + 1)
    lengths = lengths.at[source_of].add(-passed).at[receiver].add(passed)
    items = jnp.searchsorted(jnp.cumsum(lengths), jnp.arange(rows * top), side="right").astype(jnp.int32)
    grid = items.reshape(top, rows).T
    grid = grid[jax.random.permutation(jax.random.fold_in(own, 1), rows)]
    offset_by = jax.random.randint(jax.random.fold_in(own, 2), (rows, 1), 0, top)
    return jnp.take_along_axis(grid, (jnp.arange(top)[None, :] + offset_by) % top, axis=1)


def shares(count, total, limit, lean, full):
    loads = [(1 << 20) // math.isqrt(standing ** lean) + 1 for standing in range(1, count + 1)]
    largest = limit if full else min(limit, max(-(-total // count), total * loads[0] // sum(loads)))
    least = 1 if total - largest >= count - 1 else 0
    given, rest = [largest] + [least] * (count - 1), total - largest - least * (count - 1)
    while rest > 0:
        candidates = [i for i in range(1, count) if given[i] < largest] or [i for i in range(1, count) if given[i] < limit]
        mass, left = sum([loads[i] for i in candidates]), rest
        for i in candidates:
            more = min(limit - given[i], max(1, left * loads[i] // mass), rest)
            given[i] = given[i] + more
            rest = rest - more
    return np.array(given)


def bell_draw(key, shape, width, limit, cuts=(), kind=jnp.bfloat16):
    factor_of = steps_of(key, shape, cuts, -0.22, 0.18) if cuts else 1.0
    entries = jax.random.normal(key, shape, jnp.float32) * width * factor_of
    return jnp.minimum(jnp.maximum(entries, -limit), limit).astype(kind)


def setup_inputs(seed: int = 0) -> dict:
    splits = jax.random.split(jax.random.key(seed), 8)
    tokens = bell_draw(splits[0], (TOKENS, D), 1.0, 6.0, ((0, 256),))
    cotangent = bell_draw(splits[1], (TOKENS, D), 1.0, 6.0, ((0, 256),))
    expert_ids_keys = jax.random.split(jax.random.fold_in(splits[2], 1), TOKENS // TOK_DEV)
    expert_ids_turns = jax.random.permutation(jax.random.fold_in(splits[2], 3), TOKENS // TOK_DEV)
    expert_ids = jax.vmap(lambda own, number: deal_out(jax.random.fold_in(splits[2], 2), own, number, TOK_DEV, EXPERTS, TOPK, CAP, 2))(expert_ids_keys, expert_ids_turns).reshape((TOKENS, TOPK))
    gates = jnp.clip(0.19921875 + 1.3007812 * jax.random.uniform(splits[3], (TOKENS, TOPK), jnp.float32) ** steps_of(splits[3], (TOKENS, TOPK), ((0, 256),), -0.2, 0.2), 0.19921875, 1.5).astype(jnp.bfloat16)
    gate_weight = bell_draw(splits[4], (EXPERTS, D, H), D ** -0.5, 0.09375, ((0, 64), (2, 4)))
    up_weight = bell_draw(splits[5], (EXPERTS, D, H), D ** -0.5, 0.09375, ((0, 64), (2, 4)))
    down_weight = bell_draw(splits[6], (EXPERTS, H, D), H ** -0.5, 0.21875, ((0, 64), (1, 4)))
    return {"tokens": tokens, "cotangent": cotangent, "expert_ids": expert_ids, "gates": gates, "gate_weight": gate_weight, "up_weight": up_weight, "down_weight": down_weight}


def reference(tokens, cotangent, expert_ids, gates, gate_weight, up_weight, down_weight):
    rows_dev = TOK_DEV * TOPK
    quarter = H // N_REP
    routed = DEVICES * CAP
    total_rows = TOKENS * TOPK
    flat = expert_ids.reshape(-1).astype(jnp.int32)
    blocks = flat.reshape(DEVICES, rows_dev)
    onehot = (blocks[:, :, None] == jnp.arange(EXPERTS, dtype=jnp.int32)[None, None, :]).astype(jnp.int32)
    ranks = jnp.sum((jnp.cumsum(onehot, axis=1) - 1) * onehot, axis=2).reshape(-1)
    source = jnp.arange(total_rows, dtype=jnp.int32) // rows_dev
    slots = ((flat * DEVICES + source) * CAP + ranks).astype(jnp.int32)
    table = jnp.full((EXPERTS * routed,), -1, jnp.int32).at[slots].set(jnp.arange(total_rows, dtype=jnp.int32))
    table = table.reshape(EXPERTS, routed)
    flat_gates = gates.reshape(-1)

    def expert_step(operands):
        index, gate_mat, up_mat, down_mat = operands
        live = index >= 0
        safe = jnp.where(live, index, 0)
        token_rows = safe // TOPK
        inputs = jnp.where(live[:, None], tokens[token_rows], jnp.zeros((), jnp.bfloat16))
        cotan = jnp.where(live[:, None], cotangent[token_rows], jnp.zeros((), jnp.bfloat16))
        weight = jnp.where(live, flat_gates[safe].astype(jnp.float32), jnp.float32(0.0))[:, None]
        gate_pre = jnp.dot(inputs, gate_mat, preferred_element_type=jnp.float32)
        up_pre = jnp.dot(inputs, up_mat, preferred_element_type=jnp.float32)
        logistic = jax.nn.sigmoid(gate_pre)
        activated = gate_pre * logistic
        hidden = (activated * up_pre).astype(jnp.bfloat16)
        hidden_grad = jnp.dot(cotan, down_mat.T, preferred_element_type=jnp.float32)
        gate_part = jnp.sum((hidden.astype(jnp.float32) * hidden_grad).reshape(routed, N_REP, quarter), axis=2)
        gate_part = lax.optimization_barrier(gate_part.astype(jnp.bfloat16)).astype(jnp.float32)
        gate_total = jnp.sum(gate_part, axis=1).astype(jnp.bfloat16)
        weighted = hidden_grad * weight
        pre_grad = (weighted * up_pre * logistic * (1.0 + gate_pre * (1.0 - logistic))).astype(jnp.bfloat16)
        up_grad = (weighted * activated).astype(jnp.bfloat16)
        scaled_cot = (cotan.astype(jnp.float32) * weight).astype(jnp.bfloat16)
        down_grad = jnp.dot(hidden.T, scaled_cot, preferred_element_type=jnp.float32).astype(jnp.bfloat16)
        gate_grad = jnp.dot(inputs.T, pre_grad, preferred_element_type=jnp.float32).astype(jnp.bfloat16)
        upper_grad = jnp.dot(inputs.T, up_grad, preferred_element_type=jnp.float32).astype(jnp.bfloat16)
        part = jnp.einsum("mqh,dqh->qmd", pre_grad.astype(jnp.float32).reshape(routed, N_REP, quarter),
                          gate_mat.astype(jnp.float32).reshape(D, N_REP, quarter))
        part = part + jnp.einsum("mqh,dqh->qmd", up_grad.astype(jnp.float32).reshape(routed, N_REP, quarter),
                                 up_mat.astype(jnp.float32).reshape(D, N_REP, quarter))
        part = lax.optimization_barrier(part.astype(jnp.bfloat16)).astype(jnp.float32)
        row_grad = jnp.sum(part, axis=0).astype(jnp.bfloat16)
        return row_grad, gate_total, gate_grad, upper_grad, down_grad

    results = lax.map(expert_step, (table, gate_weight, up_weight, down_weight))
    row_all = results[0].reshape(EXPERTS * routed, D)
    gates_all = results[1].reshape(-1)
    per_row = row_all[slots]
    token_grad = jnp.sum(per_row.astype(jnp.float32).reshape(TOKENS, TOPK, D), axis=1).astype(jnp.bfloat16)
    gates_grad = gates_all[slots].reshape(TOKENS, TOPK)
    return token_grad, gates_grad, results[2], results[3], results[4]
```

```python
import functools

import jax
import jax.numpy as jnp
from jax import lax
from jax.experimental import pallas as pl
from jax.experimental.pallas import tpu as pltpu
from jax.sharding import PartitionSpec as P

MESH = pl.DeviceIdType.MESH
F32, BF16 = jnp.float32, jnp.bfloat16

DZ = (0, 1, 2, 6, 3, 5, 4, 7)
NC = 8
NM = 8
CAP = 4
NQ = 4
RB = NM * NQ * CAP
HR = RB // 2
QW = 1024
HID = 192
SLOTS = 3


def pick(index, table):
    return sum(jnp.where(index == k, v, 0) for k, v in enumerate(table) if v)


def kernel(
    tok_ref, cot_ref, ids_ref, g_ref, wg_ref, wu_ref, wd_ref,
    tgrad_ref, ggrad_ref, dg_ref, du_ref, dd_ref,
    land, pack, stack, perm, wnat, wtr, part, transit, full, gpart, grecv, ret, back, acts, dout,
    a2a_s, a2a_r, ag1_s, ag1_r, ag2_s, ag2_r, rs1_s, rs1_r, rs2_s, rs2_r, gt_s, gt_r, ret_s, ret_r, w_sem, o_sem,
):
    rep, ep = lax.axis_index("rep"), lax.axis_index("ep")
    my_y, my_z, my_c = ep // 16, (ep // 2) % 8, ep % 2
    right, left, across = (rep + 1) % 4, (rep + 3) % 4, (rep + 2) % 4

    loads = [
        pltpu.make_async_copy(src.at[0], wnat.at[k], w_sem.at[k])
        for k, src in enumerate((wg_ref, wu_ref, wd_ref))
    ]
    for load in loads:
        load.start()

    barrier = pltpu.get_barrier_semaphore()

    def greet(k, carry):
        pl.semaphore_signal(barrier, inc=1, device_id=(rep, (ep + k) % 64), device_id_type=MESH)
        return carry

    lax.fori_loop(1, 64, greet, 0)
    for peer in (left, right, across):
        pl.semaphore_signal(barrier, inc=1, device_id=(peer, ep), device_id_type=MESH)

    ids = ids_ref[...].astype(F32)
    by_lane = jnp.broadcast_to(ids, (128, 128))
    by_row = by_lane.T
    a = lax.broadcasted_iota(jnp.int32, (128, 128), 0)
    b = lax.broadcasted_iota(jnp.int32, (128, 128), 1)
    same = jnp.where(by_lane == by_row, 1, 0)
    rank = jnp.sum(jnp.where(a < b, same, 0), axis=0, keepdims=True)
    expert = ids_ref[...]
    dy = ((expert >> 4) - my_y) & 3
    dz = (((expert >> 1) & 7) - my_z) & 7
    dc = (expert - my_c) & 1
    chunk_of = sum(jnp.where(dz == d, k, 0) for k, d in enumerate(DZ) if k)
    pos = (chunk_of * NM + dy * 2 + dc) * CAP + rank

    gates_row = g_ref[...].astype(F32)
    gates_col = jnp.broadcast_to(gates_row, (128, 128)).T[:, :1]
    for q in range(NQ):
        stack[0, q * 128 : (q + 1) * 128, :] = tok_ref[:, q * QW : (q + 1) * QW]
        cot = cot_ref[:, q * QW : (q + 1) * QW].astype(F32)
        stack[1, q * 128 : (q + 1) * 128, :] = (cot * gates_col).astype(BF16)

    pr = lax.broadcasted_iota(jnp.int32, (256, 256), 0)
    pc = lax.broadcasted_iota(jnp.int32, (256, 256), 1)
    perm[0] = jnp.where(pc == ((pr & 63) >> 2) * 16 + (pr >> 6) * 4 + (pr & 3), 1.0, 0.0).astype(BF16)
    perm[1] = jnp.where(pr == ((pc & 63) >> 2) * 16 + (pc >> 6) * 4 + (pc & 3), 1.0, 0.0).astype(BF16)

    def partner(c, m, sign):
        z = (my_z + sign * pick(c, DZ) + 8) % 8
        y = (my_y + sign * (m // 2) + 4) % 4
        return y * 16 + z * 2 + (my_c + m) % 2

    sr = lax.broadcasted_iota(jnp.int32, (RB, 512), 0)
    sc = lax.broadcasted_iota(jnp.int32, (RB, 512), 1)
    slot_of_row = (sr >> 4) * CAP + (sr & 3)
    quarter_ok = ((sr >> 2) & 3) == (sc >> 7)
    pos4 = jnp.concatenate([pos] * NQ, axis=1)

    def fill(c):
        onehot = jnp.where(quarter_ok & (pos4 - c * (NM * CAP) == slot_of_row), 1.0, 0.0).astype(BF16)
        for k in range(2):
            pack[k, c] = jnp.dot(onehot, stack[k], preferred_element_type=F32).astype(BF16)

    def send(c, m):
        rows = pl.ds(pl.multiple_of(m * 16, 16), 16)
        for k in range(2):
            pltpu.make_async_remote_copy(
                src_ref=pack.at[k, c, rows],
                dst_ref=land.at[k, c, 0, rows],
                send_sem=a2a_s.at[k, c],
                recv_sem=a2a_r.at[k, c],
                device_id=(rep, partner(c, m, 1)),
                device_id_type=MESH,
            ).start()

    fill(0)
    pl.semaphore_wait(barrier, 66)
    own_copies = [
        pltpu.make_async_copy(pack.at[k, 0, pl.ds(0, 16)], land.at[k, 0, 0, pl.ds(0, 16)], a2a_r.at[k, 0])
        for k in range(2)
    ]
    for copy in own_copies:
        copy.start()

    def send_first(m, carry):
        send(0, m)
        return carry

    lax.fori_loop(1, NM, send_first, 0)

    def send_chunk(c, carry):
        fill(c)

        def one(m, inner):
            send(c, m)
            return inner

        lax.fori_loop(0, NM, one, 0)
        return carry

    lax.fori_loop(1, NC, send_chunk, 0)

    for load in loads:
        load.wait()

    def turn(j, carry):
        cols = pl.ds(pl.multiple_of(j * 512, 512), 512)
        for k in range(3):
            wtr[k, cols, :] = wnat[k, :, cols].T
        return carry

    lax.fori_loop(0, 8, turn, 0)

    def ring(src, dst, send_sem, recv_sem, peer):
        return pltpu.make_async_remote_copy(
            src_ref=src, dst_ref=dst, send_sem=send_sem, recv_sem=recv_sem,
            device_id=(peer, ep), device_id_type=MESH,
        )

    def gather_one(k, c):
        own = land.at[k, c, 0, pl.ds(0, RB)]
        return (
            ring(own, land.at[k, c, 0, pl.ds(RB, RB)], ag1_s.at[k, 0, c], ag1_r.at[k, 0, c], right),
            ring(own, land.at[k, c, 1, pl.ds(0, RB)], ag1_s.at[k, 1, c], ag1_r.at[k, 1, c], left),
        )

    def gather_two(k, c):
        return (
            ring(
                land.at[k, c, 0, pl.ds(RB, HR)], land.at[k, c, 1, pl.ds(RB, HR)],
                ag2_s.at[k, 0, c], ag2_r.at[k, 0, c], right,
            ),
            ring(
                land.at[k, c, 1, pl.ds(HR, HR)], land.at[k, c, 1, pl.ds(RB + HR, HR)],
                ag2_s.at[k, 1, c], ag2_r.at[k, 1, c], left,
            ),
        )

    def scatter_one(c):
        p = c % SLOTS
        return (
            ring(part.at[p, 3, pl.ds(0, HR)], transit.at[0, c], rs1_s.at[0, c], rs1_r.at[0, c], right),
            ring(part.at[p, 3, pl.ds(HR, HR)], transit.at[1, c], rs1_s.at[1, c], rs1_r.at[1, c], left),
        )

    def scatter_two(c):
        p = c % SLOTS
        return (
            ring(part.at[p, 2], full.at[0, c], rs2_s.at[0, c], rs2_r.at[0, c], right),
            ring(part.at[p, 1], full.at[1, c], rs2_s.at[1, c], rs2_r.at[1, c], left),
        )

    def gate_copies(c):
        return [
            ring(gpart.at[c], grecv.at[j, c], gt_s.at[j, c], gt_r.at[j, c], peer)
            for j, peer in enumerate((right, left, across))
        ]

    def step_gather_one(c):
        for k in range(2):
            whole = land.at[k, c, 0, pl.ds(0, RB)]
            pltpu.make_async_copy(whole, whole, a2a_r.at[k, c]).wait()
            for copy in gather_one(k, c):
                copy.start()

    def step_gather_two(c):
        for k in range(2):
            firsts, seconds = gather_one(k, c), gather_two(k, c)
            for first, second in zip(firsts, seconds):
                first.wait_recv()
                second.start()

    def step_compute(c):
        p = c % SLOTS
        for k in range(2):
            for copy in gather_two(k, c):
                copy.wait_recv()
                copy.wait_send()
            for copy in gather_one(k, c):
                copy.wait_send()
        rows = []
        for k in range(2):
            for g in range(2):
                land[k, c, g] = jnp.dot(perm[0], land[k, c, g], preferred_element_type=F32).astype(BF16)

        def quarter(k, q):
            return jnp.concatenate([land[k, c, g, q * 64 : (q + 1) * 64, :] for g in range(2)], axis=0)

        def project(k, w):
            return sum(
                jnp.dot(quarter(k, q), wtr[w, q * QW : (q + 1) * QW, :], preferred_element_type=F32)
                for q in range(NQ)
            )

        gate_pre, up_pre, weighted = project(0, 0), project(0, 1), project(1, 2)
        logistic = jax.nn.sigmoid(gate_pre)
        activated = gate_pre * logistic
        hidden = (activated * up_pre).astype(BF16)
        pre_grad = (weighted * up_pre * logistic * (1.0 + gate_pre * (1.0 - logistic))).astype(BF16)
        up_grad = (weighted * activated).astype(BF16)
        gate_sum = jnp.sum(hidden.astype(F32) * weighted, axis=1, keepdims=True)
        gpart[c] = jnp.broadcast_to(gate_sum, (128, 128)).T[:8, :]
        cols = pl.ds(pl.multiple_of(c * 128, 128), 128)
        acts[0, :, cols] = pre_grad.T
        acts[1, :, cols] = up_grad.T
        acts[2, :, cols] = hidden.T
        for copy in gate_copies(c):
            copy.start()
        parts = []
        for q in range(NQ):
            both = jnp.dot(pre_grad, wnat[0, :, q * QW : (q + 1) * QW], preferred_element_type=F32)
            both = both + jnp.dot(up_grad, wnat[1, :, q * QW : (q + 1) * QW], preferred_element_type=F32)
            parts.append(both.astype(BF16))
        for g in (1, 0):
            stacked = jnp.concatenate([piece[g * 64 : (g + 1) * 64] for piece in parts], axis=0)
            message = jnp.dot(perm[1], stacked, preferred_element_type=F32).astype(BF16)
            part[p, 2 * g] = message[:RB]
            part[p, 2 * g + 1] = message[RB:]
        for copy in scatter_one(c):
            copy.start()

    def step_scatter_two(c):
        p = c % SLOTS
        ones, twos = scatter_one(c), scatter_two(c)
        for j, (rel, rows) in enumerate(((2, pl.ds(0, HR)), (1, pl.ds(HR, HR)))):
            ones[j].wait_recv()
            total = part[p, rel, rows, :].astype(F32) + transit[j, c].astype(F32)
            part[p, rel, rows, :] = total.astype(BF16)
            twos[j].start()

    gr = lax.broadcasted_iota(jnp.int32, (RB, 128), 0)
    gl = lax.broadcasted_iota(jnp.int32, (RB, 128), 1)
    slot_lane = (gr >> 4) * CAP + (gr & 3)

    def ret_copy(c, m):
        rows = pl.ds(pl.multiple_of(m * 16, 16), 16)
        return pltpu.make_async_remote_copy(
            src_ref=ret.at[c, rows],
            dst_ref=back.at[c, rows],
            send_sem=ret_s.at[c],
            recv_sem=ret_r.at[c],
            device_id=(rep, partner(c, m, -1)),
            device_id_type=MESH,
        )

    def step_return(c):
        p = c % SLOTS
        for copy in scatter_two(c):
            copy.wait_recv()
            copy.wait_send()
        for copy in scatter_one(c):
            copy.wait_send()
        for copy in gate_copies(c):
            copy.wait()
        total = part[p, 0].astype(F32) + full[0, c].astype(F32) + full[1, c].astype(F32)
        ret[c, :, :QW] = total.astype(BF16)
        gate = jnp.where(gl == slot_lane, gpart[c, :1, :], 0.0)
        gate = gate + jnp.where(gl == slot_lane + 64, grecv[0, c, :1, :], 0.0)
        gate = gate + jnp.where(gl == slot_lane + 32, grecv[1, c, :1, :], 0.0)
        gate = gate + jnp.where(gl == slot_lane + 96, grecv[2, c, :1, :], 0.0)
        gate = jnp.sum(gate, axis=1, keepdims=True)
        ret[c, :, QW:] = jnp.broadcast_to(gate, (RB, 128)).astype(BF16)

        @pl.when(c == 0)
        def _():
            pltpu.make_async_copy(ret.at[0, pl.ds(0, 16)], back.at[0, pl.ds(0, 16)], ret_r.at[0]).start()

        def one(m, carry):
            ret_copy(c, m).start()
            return carry

        lax.fori_loop(jnp.where(c == 0, 1, 0), NM, one, 0)

    def step(t, carry):
        pl.when(t < NC)(lambda: step_gather_one(t))
        pl.when((t >= 1) & (t < NC + 1))(lambda: step_gather_two(t - 1))
        pl.when((t >= 2) & (t < NC + 2))(lambda: step_compute(t - 2))
        pl.when((t >= 3) & (t < NC + 3))(lambda: step_scatter_two(t - 3))
        pl.when((t >= 4) & (t < NC + 4))(lambda: step_return(t - 4))
        return carry

    lax.fori_loop(0, NC + 4, step, 0)

    def weight_grads(j, carry):
        q, col = j // 4, pl.ds(pl.multiple_of((j % 4) * 256, 256), 256)
        out = pl.ds(pl.multiple_of(j * 256, 256), 256)
        rows = pl.ds(pl.multiple_of(q * 64, 64), 64)
        x = land[0, :, :, rows, col].reshape(NC * 128, 256)
        cot = land[1, :, :, rows, col].reshape(NC * 128, 256)
        dout[0, :, out] = jnp.dot(acts[0], x, preferred_element_type=F32).astype(BF16)
        dout[1, :, out] = jnp.dot(acts[1], x, preferred_element_type=F32).astype(BF16)
        dout[2, :, out] = jnp.dot(acts[2], cot, preferred_element_type=F32).astype(BF16)
        return carry

    lax.fori_loop(0, 16, weight_grads, 0)
    stores = [
        pltpu.make_async_copy(dout.at[k], dst.at[0], o_sem.at[k])
        for k, dst in enumerate((dg_ref, du_ref, dd_ref))
    ]
    for store in stores:
        store.start()

    pos_col = jnp.broadcast_to(pos.astype(F32), (128, 128)).T[:, :1].astype(jnp.int32)
    mr = lax.broadcasted_iota(jnp.int32, (128, NC * RB), 1)
    hit = (mr >> 4) * CAP + (mr & 3) == pos_col
    for c in range(NC):
        pltpu.make_async_copy(back.at[c], back.at[c], ret_r.at[c]).wait()
    rows_back = back[...].reshape(NC * RB, QW + 128)
    for q in range(NQ):
        take = jnp.where(hit & (((mr >> 2) & 3) == q), 1.0, 0.0).astype(BF16)
        tgrad_ref[:, q * QW : (q + 1) * QW] = jnp.dot(
            take, rows_back[:, :QW], preferred_element_type=F32
        ).astype(BF16)
        if q == 0:
            gate = jnp.dot(take, rows_back[:, QW:], preferred_element_type=F32)
            ggrad_ref[...] = (gate.T[:1, :] / gates_row).astype(BF16)

    skip = pl.ds(16, RB - 16)
    for c in range(NC):
        rows = skip if c == 0 else pl.ds(0, RB)
        for k in range(2):
            pltpu.make_async_copy(pack.at[k, c, rows], pack.at[k, c, rows], a2a_s.at[k, c]).wait()
        pltpu.make_async_copy(ret.at[c, rows], ret.at[c, rows], ret_s.at[c]).wait()
    for store in stores:
        store.wait()


def shards(tokens, cotangent, expert_ids, gates, gate_weight, up_weight, down_weight):
    rows, width = tokens.shape
    vmem, hbm = pl.BlockSpec(memory_space=pltpu.VMEM), pl.BlockSpec(memory_space=pl.ANY)
    dma = pltpu.SemaphoreType.DMA
    out = pl.pallas_call(
        kernel,
        out_shape=(
            jax.ShapeDtypeStruct((rows, width), BF16),
            jax.ShapeDtypeStruct((1, rows), BF16),
            jax.ShapeDtypeStruct((1, HID, width), BF16),
            jax.ShapeDtypeStruct((1, HID, width), BF16),
            jax.ShapeDtypeStruct((1, HID, width), BF16),
        ),
        in_specs=[vmem] * 4 + [hbm] * 3,
        out_specs=(vmem, vmem, hbm, hbm, hbm),
        scratch_shapes=[
            pltpu.VMEM((2, NC, 2, 2 * RB, QW), BF16),
            pltpu.VMEM((2, NC, RB, QW), BF16),
            pltpu.VMEM((2, NQ * 128, QW), BF16),
            pltpu.VMEM((2, 256, 256), BF16),
            pltpu.VMEM((3, HID, width), BF16),
            pltpu.VMEM((3, width, HID), BF16),
            pltpu.VMEM((SLOTS, 4, RB, QW), BF16),
            pltpu.VMEM((2, NC, HR, QW), BF16),
            pltpu.VMEM((2, NC, RB, QW), BF16),
            pltpu.VMEM((NC, 8, 128), F32),
            pltpu.VMEM((3, NC, 8, 128), F32),
            pltpu.VMEM((NC, RB, QW + 128), BF16),
            pltpu.VMEM((NC, RB, QW + 128), BF16),
            pltpu.VMEM((3, HID, NC * 128), BF16),
            pltpu.VMEM((3, HID, width), BF16),
            dma((2, NC)), dma((2, NC)),
            dma((2, 2, NC)), dma((2, 2, NC)), dma((2, 2, NC)), dma((2, 2, NC)),
            dma((2, NC)), dma((2, NC)), dma((2, NC)), dma((2, NC)),
            dma((3, NC)), dma((3, NC)),
            dma((NC,)), dma((NC,)),
            dma((3,)), dma((3,)),
        ],
        compiler_params=pltpu.CompilerParams(
            collective_id=0, has_side_effects=True, vmem_limit_bytes=62 * 1024 * 1024
        ),
    )(
        tokens,
        cotangent,
        expert_ids.reshape(1, rows),
        gates.reshape(1, rows),
        jnp.transpose(gate_weight, (0, 2, 1)),
        jnp.transpose(up_weight, (0, 2, 1)),
        down_weight,
    )
    token_grad, gates_grad, gate_grad, upper_grad, down_grad = out
    return (
        token_grad,
        gates_grad.reshape(rows, 1),
        jnp.transpose(gate_grad, (0, 2, 1)),
        jnp.transpose(upper_grad, (0, 2, 1)),
        down_grad,
    )


def solution(mesh):
    in_specs = (
        P(("rep", "ep"), None),
        P(("rep", "ep"), None),
        P(("rep", "ep"), None),
        P(("rep", "ep"), None),
        P("ep", None, "rep"),
        P("ep", None, "rep"),
        P("ep", "rep", None),
    )
    out_specs = (
        P(("rep", "ep"), None),
        P(("rep", "ep"), None),
        P("ep", None, "rep"),
        P("ep", None, "rep"),
        P("ep", "rep", None),
    )
    return jax.shard_map(shards, mesh=mesh, in_specs=in_specs, out_specs=out_specs, check_vma=False)
```

```python
import jax
import jax.numpy as jnp
from jax import lax
from jax.experimental import pallas as pl
from jax.experimental.pallas import tpu as pltpu
from jax.sharding import PartitionSpec as P

MESH = pl.DeviceIdType.MESH
F32, BF16 = jnp.float32, jnp.bfloat16

DZ = (0, 7, 2, 5, 4, 3, 6, 1)
NC = 16
NM = 4
CAP = 4
NQ = 4
RB = NM * NQ * CAP
HR = RB // 2
QW = 1024
BW = QW + 128
HID = 192
SLOTS = 3
ROWS = NC * NM * CAP


def pick(index, table):
    return sum(jnp.where(index == k, v, 0) for k, v in enumerate(table) if v)


def positions(ids_ref, my_y, my_z, my_c):
    ids = ids_ref[...].astype(F32)
    by_lane = jnp.broadcast_to(ids, (128, 128))
    by_row = by_lane.T
    a = lax.broadcasted_iota(jnp.int32, (128, 128), 0)
    b = lax.broadcasted_iota(jnp.int32, (128, 128), 1)
    same = jnp.where(by_lane == by_row, 1, 0)
    rank = jnp.sum(jnp.where(a < b, same, 0), axis=0, keepdims=True)
    expert = ids_ref[...]
    dy = ((expert >> 4) - my_y) & 3
    dz = (((expert >> 1) & 7) - my_z) & 7
    dc = (expert - my_c) & 1
    at_z = sum(jnp.where(dz == d, k, 0) for k, d in enumerate(DZ) if k)
    return ((at_z * 2 + dc) * NM + dy) * CAP + rank


def kernel(
    tok_ref, cot_ref, ids_ref, g_ref, wg_ref, wu_ref, wd_ref,
    back, dg_ref, du_ref, dd_ref,
    land, pack, stack, perm, wnat, wtr, part, transit, full, gpart, grecv, ret, acts, acts_t, dout,
    a2a_s, a2a_r, ag1_s, ag1_r, ag2_s, ag2_r, rs1_s, rs1_r, rs2_s, rs2_r, gt_s, gt_r, ret_s, ret_r, w_sem, o_sem,
):
    rep, ep = lax.axis_index("rep"), lax.axis_index("ep")
    my_y, my_z, my_c = ep // 16, (ep // 2) % 8, ep % 2
    right, left, across = (rep + 1) % 4, (rep + 3) % 4, (rep + 2) % 4

    loads = [
        pltpu.make_async_copy(src.at[0], wnat.at[k], w_sem.at[k])
        for k, src in enumerate((wg_ref, wu_ref, wd_ref))
    ]
    for load in loads:
        load.start()

    barrier = pltpu.get_barrier_semaphore()

    def greet(k, carry):
        pl.semaphore_signal(barrier, inc=1, device_id=(rep, (ep + k) % 64), device_id_type=MESH)
        return carry

    lax.fori_loop(1, 64, greet, 0)
    for peer in (left, right, across):
        pl.semaphore_signal(barrier, inc=1, device_id=(peer, ep), device_id_type=MESH)

    pos = positions(ids_ref, my_y, my_z, my_c)
    gates_row = g_ref[...].astype(F32)
    gates_col = jnp.broadcast_to(gates_row, (128, 128)).T[:, :1]
    for q in range(NQ):
        stack[0, q * 128 : (q + 1) * 128, :] = tok_ref[:, q * QW : (q + 1) * QW]
        cot = cot_ref[:, q * QW : (q + 1) * QW].astype(F32)
        stack[1, q * 128 : (q + 1) * 128, :] = (cot * gates_col).astype(BF16)

    pr = lax.broadcasted_iota(jnp.int32, (256, 256), 0)
    pc = lax.broadcasted_iota(jnp.int32, (256, 256), 1)
    perm[0] = jnp.where(pc == ((pr & 63) >> 2) * 16 + (pr >> 6) * 4 + (pr & 3), 1.0, 0.0).astype(BF16)
    perm[1] = jnp.where(pr == ((pc & 63) >> 2) * 16 + (pc >> 6) * 4 + (pc & 3), 1.0, 0.0).astype(BF16)

    def partner(c, m, sign):
        z = (my_z + sign * pick(c // 2, DZ) + 8) % 8
        y = (my_y + sign * m + 4) % 4
        return y * 16 + z * 2 + (my_c + c) % 2

    sr = lax.broadcasted_iota(jnp.int32, (2 * RB, 512), 0)
    sc = lax.broadcasted_iota(jnp.int32, (2 * RB, 512), 1)
    slot_of_row = (sr >> 4) * CAP + (sr & 3)
    quarter_ok = ((sr >> 2) & 3) == (sc >> 7)
    pos4 = jnp.concatenate([pos] * NQ, axis=1)

    def fill(j, carry):
        onehot = jnp.where(quarter_ok & (pos4 - j * (2 * NM * CAP) == slot_of_row), 1.0, 0.0).astype(BF16)
        for k in range(2):
            rows = jnp.dot(onehot, stack[k], preferred_element_type=F32).astype(BF16)
            pack[k, 2 * j] = rows[:RB]
            pack[k, 2 * j + 1] = rows[RB:]
        return carry

    lax.fori_loop(0, NC // 2, fill, 0)

    def send(c, m):
        rows = pl.ds(pl.multiple_of(m * 16, 16), 16)
        for k in range(2):
            pltpu.make_async_remote_copy(
                src_ref=pack.at[k, c, rows],
                dst_ref=land.at[k, c, rows],
                send_sem=a2a_s.at[k, c],
                recv_sem=a2a_r.at[k, c],
                device_id=(rep, partner(c, m, 1)),
                device_id_type=MESH,
            ).start()

    def send_chunk(c, carry):
        def one(m, inner):
            send(c, m)
            return inner

        lax.fori_loop(jnp.where(c == 0, 1, 0), NM, one, 0)
        return carry

    for load in loads:
        load.wait()

    def turn(j, carry):
        cols = pl.ds(pl.multiple_of(j * 512, 512), 512)
        for k in range(3):
            wtr[k, cols, :] = wnat[k, :, cols].T
        return carry

    lax.fori_loop(0, 8, turn, 0)

    pl.semaphore_wait(barrier, 66)
    for k in range(2):
        pltpu.make_async_copy(pack.at[k, 0, pl.ds(0, 16)], land.at[k, 0, pl.ds(0, 16)], a2a_r.at[k, 0]).start()
    lax.fori_loop(0, 4, send_chunk, 0)

    def ring(src, dst, send_sem, recv_sem, peer):
        return pltpu.make_async_remote_copy(
            src_ref=src, dst_ref=dst, send_sem=send_sem, recv_sem=recv_sem,
            device_id=(peer, ep), device_id_type=MESH,
        )

    def gather_one(k, c):
        own = land.at[k, c, pl.ds(0, RB)]
        return (
            ring(own, land.at[k, c, pl.ds(RB, RB)], ag1_s.at[k, 0, c], ag1_r.at[k, 0, c], right),
            ring(own, land.at[k, c, pl.ds(2 * RB, RB)], ag1_s.at[k, 1, c], ag1_r.at[k, 1, c], left),
        )

    def gather_two(k, c):
        return (
            ring(
                land.at[k, c, pl.ds(RB, HR)], land.at[k, c, pl.ds(3 * RB, HR)],
                ag2_s.at[k, 0, c], ag2_r.at[k, 0, c], right,
            ),
            ring(
                land.at[k, c, pl.ds(2 * RB + HR, HR)], land.at[k, c, pl.ds(3 * RB + HR, HR)],
                ag2_s.at[k, 1, c], ag2_r.at[k, 1, c], left,
            ),
        )

    def scatter_one(c):
        p = c % SLOTS
        return (
            ring(part.at[p, 3, pl.ds(0, HR)], transit.at[0, c], rs1_s.at[0, c], rs1_r.at[0, c], right),
            ring(part.at[p, 3, pl.ds(HR, HR)], transit.at[1, c], rs1_s.at[1, c], rs1_r.at[1, c], left),
        )

    def scatter_two(c):
        p = c % SLOTS
        return (
            ring(part.at[p, 2], full.at[0, c], rs2_s.at[0, c], rs2_r.at[0, c], right),
            ring(part.at[p, 1], full.at[1, c], rs2_s.at[1, c], rs2_r.at[1, c], left),
        )

    def gate_copies(c):
        return [
            ring(gpart.at[c], grecv.at[j, c], gt_s.at[j, c], gt_r.at[j, c], peer)
            for j, peer in enumerate((right, left, across))
        ]

    def step_gather_one(c):
        for k in range(2):
            whole = land.at[k, c, pl.ds(0, RB)]
            pltpu.make_async_copy(whole, whole, a2a_r.at[k, c]).wait()
            for copy in gather_one(k, c):
                copy.start()

    def step_gather_two(c):
        for k in range(2):
            firsts, seconds = gather_one(k, c), gather_two(k, c)
            for first, second in zip(firsts, seconds):
                first.wait_recv()
                second.start()

    def step_compute(c):
        p = c % SLOTS
        for k in range(2):
            for copy in gather_two(k, c):
                copy.wait_recv()
                copy.wait_send()
            for copy in gather_one(k, c):
                copy.wait_send()
        for k in range(2):
            land[k, c] = jnp.dot(perm[0], land[k, c], preferred_element_type=F32).astype(BF16)

        def project(k, w):
            return sum(
                jnp.dot(land[k, c, q * 64 : (q + 1) * 64, :], wtr[w, q * QW : (q + 1) * QW, :], preferred_element_type=F32)
                for q in range(NQ)
            )

        gate_pre, up_pre, weighted = project(0, 0), project(0, 1), project(1, 2)
        logistic = jax.nn.sigmoid(gate_pre)
        activated = gate_pre * logistic
        hidden = (activated * up_pre).astype(BF16)
        pre_grad = (weighted * up_pre * logistic * (1.0 + gate_pre * (1.0 - logistic))).astype(BF16)
        up_grad = (weighted * activated).astype(BF16)
        gate_sum = jnp.sum(hidden.astype(F32) * weighted, axis=1, keepdims=True)
        gate_sum = jnp.broadcast_to(jnp.concatenate([gate_sum, gate_sum], axis=0), (128, 128))
        gpart[c] = gate_sum.T[:8, :]
        rows = pl.ds(pl.multiple_of(c * 64, 64), 64)
        acts[0, rows, :] = pre_grad
        acts[1, rows, :] = up_grad
        acts[2, rows, :] = hidden
        for copy in gate_copies(c):
            copy.start()
        parts = []
        for q in range(NQ):
            both = jnp.dot(pre_grad, wnat[0, :, q * QW : (q + 1) * QW], preferred_element_type=F32)
            both = both + jnp.dot(up_grad, wnat[1, :, q * QW : (q + 1) * QW], preferred_element_type=F32)
            parts.append(both.astype(BF16))
        message = jnp.dot(perm[1], jnp.concatenate(parts, axis=0), preferred_element_type=F32).astype(BF16)
        for rel in range(4):
            part[p, rel] = message[rel * RB : (rel + 1) * RB]
        for copy in scatter_one(c):
            copy.start()

    def step_scatter_two(c):
        p = c % SLOTS
        ones, twos = scatter_one(c), scatter_two(c)
        for j, (rel, rows) in enumerate(((2, pl.ds(0, HR)), (1, pl.ds(HR, HR)))):
            ones[j].wait_recv()
            total = part[p, rel, rows, :].astype(F32) + transit[j, c].astype(F32)
            part[p, rel, rows, :] = total.astype(BF16)
            twos[j].start()

    gr = lax.broadcasted_iota(jnp.int32, (RB, 128), 0)
    gl = lax.broadcasted_iota(jnp.int32, (RB, 128), 1)
    slot_lane = (gr >> 4) * CAP + (gr & 3)

    def ret_copy(c, m):
        rows = pl.ds(pl.multiple_of(m * 16, 16), 16)
        return pltpu.make_async_remote_copy(
            src_ref=ret.at[c, rows],
            dst_ref=back.at[c, rows],
            send_sem=ret_s.at[c],
            recv_sem=ret_r.at[c],
            device_id=(rep, partner(c, m, -1)),
            device_id_type=MESH,
        )

    def step_return(c):
        p = c % SLOTS
        for copy in scatter_two(c):
            copy.wait_recv()
            copy.wait_send()
        for copy in scatter_one(c):
            copy.wait_send()
        for copy in gate_copies(c):
            copy.wait()
        total = part[p, 0].astype(F32) + full[0, c].astype(F32) + full[1, c].astype(F32)
        ret[c, :, :QW] = total.astype(BF16)
        gate = jnp.where(gl == slot_lane, gpart[c, :1, :], 0.0)
        gate = gate + jnp.where(gl == slot_lane + 2 * NM * CAP, grecv[0, c, :1, :], 0.0)
        gate = gate + jnp.where(gl == slot_lane + NM * CAP, grecv[1, c, :1, :], 0.0)
        gate = gate + jnp.where(gl == slot_lane + 3 * NM * CAP, grecv[2, c, :1, :], 0.0)
        gate = jnp.sum(gate, axis=1, keepdims=True)
        ret[c, :, QW:] = jnp.broadcast_to(gate, (RB, 128)).astype(BF16)

        @pl.when(c == 0)
        def _():
            pltpu.make_async_copy(ret.at[0, pl.ds(0, 16)], back.at[0, pl.ds(0, 16)], ret_r.at[0]).start()

        def one(m, carry):
            ret_copy(c, m).start()
            return carry

        lax.fori_loop(jnp.where(c == 0, 1, 0), NM, one, 0)

    def weight_grads(j, carry):
        q, col = j // 4, pl.ds(pl.multiple_of((j % 4) * 256, 256), 256)
        out = pl.ds(pl.multiple_of(j * 256, 256), 256)
        rows = pl.ds(pl.multiple_of(q * 64, 64), 64)
        x = land[0, :, rows, col].reshape(NC * 64, 256)
        cot = land[1, :, rows, col].reshape(NC * 64, 256)
        dout[0, :, out] = jnp.dot(acts_t[0], x, preferred_element_type=F32).astype(BF16)
        dout[1, :, out] = jnp.dot(acts_t[1], x, preferred_element_type=F32).astype(BF16)
        dout[2, :, out] = jnp.dot(acts_t[2], cot, preferred_element_type=F32).astype(BF16)
        return carry

    def turn_acts():
        for k in range(3):
            acts_t[k] = acts[k].T

    def step(t, carry):
        pl.when(t < NC)(lambda: step_gather_one(t))
        pl.when((t >= 1) & (t < NC + 1))(lambda: step_gather_two(t - 1))
        lax.fori_loop(jnp.where(t < 2, 4 + 6 * t, NC), jnp.where(t < 2, 10 + 6 * t, NC), send_chunk, 0)
        pl.when((t >= 2) & (t < NC + 2))(lambda: step_compute(t - 2))
        pl.when((t >= 3) & (t < NC + 3))(lambda: step_scatter_two(t - 3))
        pl.when((t >= 4) & (t < NC + 4))(lambda: step_return(t - 4))
        pl.when(t == NC + 1)(turn_acts)
        first = jnp.where(t == NC + 1, 0, jnp.where(t == NC + 2, 4, 10))
        last = jnp.where(t == NC + 1, 4, jnp.where(t == NC + 2, 10, jnp.where(t == NC + 3, 16, 0)))
        lax.fori_loop(first, last, weight_grads, 0)
        return carry

    lax.fori_loop(0, NC + 4, step, 0)

    stores = [
        pltpu.make_async_copy(dout.at[k], dst.at[0], o_sem.at[k])
        for k, dst in enumerate((dg_ref, du_ref, dd_ref))
    ]
    for store in stores:
        store.start()
    skip = pl.ds(16, RB - 16)
    for c in range(NC):
        pltpu.make_async_copy(back.at[c], back.at[c], ret_r.at[c]).wait()
        rows = skip if c == 0 else pl.ds(0, RB)
        for k in range(2):
            pltpu.make_async_copy(pack.at[k, c, rows], pack.at[k, c, rows], a2a_s.at[k, c]).wait()
        pltpu.make_async_copy(ret.at[c, rows], ret.at[c, rows], ret_s.at[c]).wait()
    for store in stores:
        store.wait()


def finish(
    back_hbm, ids_ref, g_ref, dg_ref, du_ref, dd_ref,
    tgrad_ref, ggrad_ref, og_ref, ou_ref, od_ref,
    back, grads, b_sem, in_sem, out_sem,
):
    ep = lax.axis_index("ep")
    load = pltpu.make_async_copy(back_hbm, back, b_sem)
    load.start()
    fetches = [
        pltpu.make_async_copy(src.at[0], grads.at[k], in_sem.at[k]) for k, src in enumerate((dg_ref, du_ref, dd_ref))
    ]
    stores = [
        pltpu.make_async_copy(grads.at[k], dst.at[0], out_sem.at[k]) for k, dst in enumerate((og_ref, ou_ref, od_ref))
    ]
    for fetch in fetches:
        fetch.start()
    pos = positions(ids_ref, ep // 16, (ep // 2) % 8, ep % 2)
    pos_col = jnp.broadcast_to(pos.astype(F32), (128, 128)).T[:, :1].astype(jnp.int32)
    mr = lax.broadcasted_iota(jnp.int32, (128, NC * RB), 1)
    hit = (mr >> 4) * CAP + (mr & 3) == pos_col
    load.wait()
    for q in range(NQ):
        take = jnp.where(hit & (((mr >> 2) & 3) == q), 1.0, 0.0).astype(BF16)
        rows = back[:, :, :QW].reshape(NC * RB, QW)
        tgrad_ref[:, q * QW : (q + 1) * QW] = jnp.dot(take, rows, preferred_element_type=F32).astype(BF16)
        if q == 0:
            gate = jnp.dot(take, back[:, :, QW:].reshape(NC * RB, 128), preferred_element_type=F32)
            ggrad_ref[...] = (gate.T[:1, :] / g_ref[...].astype(F32)).astype(BF16)
        if q < 3:
            fetches[q].wait()
            stores[q].start()
    for store in stores:
        store.wait()


def shards(tokens, cotangent, expert_ids, gates, gate_weight, up_weight, down_weight):
    rows, width = tokens.shape
    vmem, hbm = pl.BlockSpec(memory_space=pltpu.VMEM), pl.BlockSpec(memory_space=pl.ANY)
    dma = pltpu.SemaphoreType.DMA
    ids, gates = expert_ids.reshape(1, rows), gates.reshape(1, rows)
    weight_shape = jax.ShapeDtypeStruct((1, HID, width), BF16)
    back, *grads = pl.pallas_call(
        kernel,
        out_shape=(jax.ShapeDtypeStruct((NC, RB, BW), BF16),) + (weight_shape,) * 3,
        in_specs=[vmem] * 4 + [hbm] * 3,
        out_specs=(hbm,) * 4,
        scratch_shapes=[
            pltpu.VMEM((2, NC, 4 * RB, QW), BF16),
            pltpu.VMEM((2, NC, RB, QW), BF16),
            pltpu.VMEM((2, NQ * 128, QW), BF16),
            pltpu.VMEM((2, 256, 256), BF16),
            pltpu.VMEM((3, HID, width), BF16),
            pltpu.VMEM((3, width, HID), BF16),
            pltpu.VMEM((SLOTS, 4, RB, QW), BF16),
            pltpu.VMEM((2, NC, HR, QW), BF16),
            pltpu.VMEM((2, NC, RB, QW), BF16),
            pltpu.VMEM((NC, 8, 128), F32),
            pltpu.VMEM((3, NC, 8, 128), F32),
            pltpu.VMEM((NC, RB, BW), BF16),
            pltpu.VMEM((3, NC * 64, HID), BF16),
            pltpu.VMEM((3, HID, NC * 64), BF16),
            pltpu.VMEM((3, HID, width), BF16),
            dma((2, NC)), dma((2, NC)),
            dma((2, 2, NC)), dma((2, 2, NC)), dma((2, 2, NC)), dma((2, 2, NC)),
            dma((2, NC)), dma((2, NC)), dma((2, NC)), dma((2, NC)),
            dma((3, NC)), dma((3, NC)),
            dma((NC,)), dma((NC,)),
            dma((3,)), dma((3,)),
        ],
        compiler_params=pltpu.CompilerParams(
            collective_id=0, has_side_effects=True, vmem_limit_bytes=62 * 1024 * 1024
        ),
    )(
        tokens,
        cotangent,
        ids,
        gates,
        jnp.transpose(gate_weight, (0, 2, 1)),
        jnp.transpose(up_weight, (0, 2, 1)),
        down_weight,
    )
    token_grad, gates_grad, gate_grad, upper_grad, down_grad = pl.pallas_call(
        finish,
        out_shape=(
            jax.ShapeDtypeStruct((rows, width), BF16),
            jax.ShapeDtypeStruct((1, rows), BF16),
        ) + (weight_shape,) * 3,
        in_specs=[hbm, vmem, vmem] + [hbm] * 3,
        out_specs=(vmem, vmem, hbm, hbm, hbm),
        scratch_shapes=[
            pltpu.VMEM((NC, RB, BW), BF16), pltpu.VMEM((3, HID, width), BF16), dma, dma((3,)), dma((3,)),
        ],
        compiler_params=pltpu.CompilerParams(vmem_limit_bytes=62 * 1024 * 1024),
    )(back, ids, gates, *grads)
    return (
        token_grad,
        gates_grad.reshape(rows, 1),
        jnp.transpose(gate_grad, (0, 2, 1)),
        jnp.transpose(upper_grad, (0, 2, 1)),
        down_grad,
    )


def solution(mesh):
    in_specs = (
        P(("rep", "ep"), None),
        P(("rep", "ep"), None),
        P(("rep", "ep"), None),
        P(("rep", "ep"), None),
        P("ep", None, "rep"),
        P("ep", None, "rep"),
        P("ep", "rep", None),
    )
    out_specs = (
        P(("rep", "ep"), None),
        P(("rep", "ep"), None),
        P("ep", None, "rep"),
        P("ep", None, "rep"),
        P("ep", "rep", None),
    )
    return jax.shard_map(shards, mesh=mesh, in_specs=in_specs, out_specs=out_specs, check_vma=False)
```

```python
import jax
import jax.numpy as jnp
from jax import lax
from jax.experimental import pallas as pl
from jax.experimental.pallas import tpu as pltpu
from jax.sharding import PartitionSpec as P

MESH = pl.DeviceIdType.MESH
F32, BF16 = jnp.float32, jnp.bfloat16

DZ = (0, 7, 2, 5, 4, 3, 6, 1)
NC = 16
NM = 4
CAP = 4
NQ = 4
RB = NM * NQ * CAP
HR = RB // 2
QW = 1024
EW = 512
MW = QW - EW // NQ
MAIN = NQ * MW
BW = QW + 128
HID = 192
SLOTS = 3
ROWS = NC * NM * CAP


def pick(index, table):
    return sum(jnp.where(index == k, v, 0) for k, v in enumerate(table) if v)


def positions(ids_ref, my_y, my_z, my_c):
    ids = ids_ref[...].astype(F32)
    by_lane = jnp.broadcast_to(ids, (128, 128))
    by_row = by_lane.T
    a = lax.broadcasted_iota(jnp.int32, (128, 128), 0)
    b = lax.broadcasted_iota(jnp.int32, (128, 128), 1)
    same = jnp.where(by_lane == by_row, 1, 0)
    rank = jnp.sum(jnp.where(a < b, same, 0), axis=0, keepdims=True)
    expert = ids_ref[...]
    dy = ((expert >> 4) - my_y) & 3
    dz = (((expert >> 1) & 7) - my_z) & 7
    dc = (expert - my_c) & 1
    at_z = sum(jnp.where(dz == d, k, 0) for k, d in enumerate(DZ) if k)
    return ((at_z * 2 + dc) * NM + dy) * CAP + rank


def kernel(
    tok_ref, cot_ref, ids_ref, g_ref, wg_ref, wu_ref, wd_ref,
    back, dg_ref, du_ref, dd_ref,
    land, pack, stack, eland, epack, estack, pos_own, pos_recv, perm, eperm, wnat, wtr, part, transit, full, gpart, grecv, ret, acts, acts_t, dout,
    a2a_s, a2a_r, ea2a_s, ea2a_r, raw1_s, raw1_r, raw2_s, raw2_r, pos_s, pos_r, ag1_s, ag1_r, ag2_s, ag2_r, rs1_s, rs1_r, rs2_s, rs2_r, gt_s, gt_r, ret_s, ret_r, w_sem, o_sem,
):
    rep, ep = lax.axis_index("rep"), lax.axis_index("ep")
    my_y, my_z, my_c = ep // 16, (ep // 2) % 8, ep % 2
    right, left, across = (rep + 1) % 4, (rep + 3) % 4, (rep + 2) % 4

    loads = [
        pltpu.make_async_copy(src.at[0], wnat.at[k], w_sem.at[k])
        for k, src in enumerate((wg_ref, wu_ref, wd_ref))
    ]
    for load in loads:
        load.start()

    barrier = pltpu.get_barrier_semaphore()

    def greet(k, carry):
        pl.semaphore_signal(barrier, inc=1, device_id=(rep, (ep + k) % 64), device_id_type=MESH)
        return carry

    lax.fori_loop(1, 64, greet, 0)
    for peer in (left, right, across):
        pl.semaphore_signal(barrier, inc=1, device_id=(peer, ep), device_id_type=MESH)

    pos = positions(ids_ref, my_y, my_z, my_c)
    gates_row = g_ref[...].astype(F32)
    gates_col = jnp.broadcast_to(gates_row, (128, 128)).T[:, :1]
    pos_own[...] = jnp.broadcast_to(pos.astype(F32), (8, 128))
    for q in range(NQ):
        stack[0, q * 128 : (q + 1) * 128, :] = tok_ref[:, q * MW : (q + 1) * MW]
        cot = cot_ref[:, q * MW : (q + 1) * MW].astype(F32)
        stack[1, q * 128 : (q + 1) * 128, :] = (cot * gates_col).astype(BF16)
    estack[0, :128, :] = tok_ref[:, MAIN:]
    estack[1, :128, :] = (cot_ref[:, MAIN:].astype(F32) * gates_col).astype(BF16)

    pr = lax.broadcasted_iota(jnp.int32, (256, 256), 0)
    pc = lax.broadcasted_iota(jnp.int32, (256, 256), 1)
    perm[0] = jnp.where(pc == ((pr & 63) >> 2) * 16 + (pr >> 6) * 4 + (pr & 3), 1.0, 0.0).astype(BF16)
    perm[1] = jnp.where(pr == ((pc & 63) >> 2) * 16 + (pc >> 6) * 4 + (pc & 3), 1.0, 0.0).astype(BF16)

    er = lax.broadcasted_iota(jnp.int32, (64, 64), 0)
    ec = lax.broadcasted_iota(jnp.int32, (64, 64), 1)
    eperm[...] = jnp.where(ec == ((er & 15) >> 2) * 16 + (er >> 4) * 4 + (er & 3), 1.0, 0.0).astype(BF16)

    def partner(c, m, sign):
        z = (my_z + sign * pick(c // 2, DZ) + 8) % 8
        y = (my_y + sign * m + 4) % 4
        return y * 16 + z * 2 + (my_c + c) % 2

    sr = lax.broadcasted_iota(jnp.int32, (2 * RB, 512), 0)
    sc = lax.broadcasted_iota(jnp.int32, (2 * RB, 512), 1)
    slot_of_row = (sr >> 4) * CAP + (sr & 3)
    quarter_ok = ((sr >> 2) & 3) == (sc >> 7)
    pos4 = jnp.concatenate([pos] * NQ, axis=1)

    def fill_from(source, target, places, j):
        onehot = jnp.where(quarter_ok & (places - j * (2 * NM * CAP) == slot_of_row), 1.0, 0.0).astype(BF16)
        for k in range(2):
            rows = jnp.dot(onehot, source[k], preferred_element_type=F32).astype(BF16)
            target[k, 2 * j] = rows[:RB]
            target[k, 2 * j + 1] = rows[RB:]

    def fill(j, carry):
        fill_from(stack, pack, pos4, j)
        return carry

    lax.fori_loop(0, NC // 2, fill, 0)

    def send_from(source, target, send_sem, recv_sem, c):
        def one(m, inner):
            rows = pl.ds(pl.multiple_of(m * 16, 16), 16)
            for k in range(2):
                pltpu.make_async_remote_copy(
                    src_ref=source.at[k, c, rows],
                    dst_ref=target.at[k, c, rows],
                    send_sem=send_sem.at[k, c],
                    recv_sem=recv_sem.at[k, c],
                    device_id=(rep, partner(c, m, 1)),
                    device_id_type=MESH,
                ).start()
            return inner

        lax.fori_loop(jnp.where(c == 0, 1, 0), NM, one, 0)

    def send_chunk(c, carry):
        send_from(pack, land, a2a_s, a2a_r, c)
        return carry

    def send_extra(c, carry):
        send_from(epack, eland, ea2a_s, ea2a_r, c)
        return carry

    def ring(src, dst, send_sem, recv_sem, peer):
        return pltpu.make_async_remote_copy(
            src_ref=src, dst_ref=dst, send_sem=send_sem, recv_sem=recv_sem,
            device_id=(peer, ep), device_id_type=MESH,
        )

    def raw_one(k):
        own = estack.at[k, pl.ds(0, 128)]
        return (
            ring(own, estack.at[k, pl.ds(128, 128)], raw1_s.at[k, 0], raw1_r.at[k, 0], right),
            ring(own, estack.at[k, pl.ds(256, 128)], raw1_s.at[k, 1], raw1_r.at[k, 1], left),
        )

    def raw_two(k):
        return (
            ring(
                estack.at[k, pl.ds(128, 64)], estack.at[k, pl.ds(384, 64)],
                raw2_s.at[k, 0], raw2_r.at[k, 0], right,
            ),
            ring(
                estack.at[k, pl.ds(320, 64)], estack.at[k, pl.ds(448, 64)],
                raw2_s.at[k, 1], raw2_r.at[k, 1], left,
            ),
        )

    pos_copies = [
        ring(pos_own, pos_recv.at[j], pos_s.at[j], pos_r.at[j], peer) for j, peer in enumerate((right, left, across))
    ]

    pl.semaphore_wait(barrier, 66)
    for copy in pos_copies:
        copy.start()
    for k in range(2):
        for copy in raw_one(k):
            copy.start()
    for k in range(2):
        pltpu.make_async_copy(pack.at[k, 0, pl.ds(0, 16)], land.at[k, 0, pl.ds(0, 16)], a2a_r.at[k, 0]).start()
    lax.fori_loop(0, 2, send_chunk, 0)
    for k in range(2):
        for first, second in zip(raw_one(k), raw_two(k)):
            first.wait_recv()
            second.start()

    def pack_extra():
        for k in range(2):
            for copy in raw_two(k):
                copy.wait_recv()
        for copy in pos_copies:
            copy.wait_recv()
        places = jnp.concatenate([pos_own[:1, :]] + [pos_recv[j, :1, :] for j in range(3)], axis=1).astype(jnp.int32)

        def one(j, carry):
            fill_from(estack, epack, places, j)
            return carry

        lax.fori_loop(0, NC // 2, one, 0)
        for k in range(2):
            pltpu.make_async_copy(
                epack.at[k, 0, pl.ds(0, 16)], eland.at[k, 0, pl.ds(0, 16)], ea2a_r.at[k, 0]
            ).start()

    def turn_weights():
        for load in loads:
            load.wait()

        def turn(j, carry):
            cols = pl.ds(pl.multiple_of(j * 512, 512), 512)
            for k in range(3):
                wtr[k, cols, :] = wnat[k, :, cols].T
            return carry

        lax.fori_loop(0, 8, turn, 0)

    def gather_one(k, c):
        own = land.at[k, c, pl.ds(0, RB)]
        return (
            ring(own, land.at[k, c, pl.ds(RB, RB)], ag1_s.at[k, 0, c], ag1_r.at[k, 0, c], right),
            ring(own, land.at[k, c, pl.ds(2 * RB, RB)], ag1_s.at[k, 1, c], ag1_r.at[k, 1, c], left),
        )

    def gather_two(k, c):
        return (
            ring(
                land.at[k, c, pl.ds(RB, HR)], land.at[k, c, pl.ds(3 * RB, HR)],
                ag2_s.at[k, 0, c], ag2_r.at[k, 0, c], right,
            ),
            ring(
                land.at[k, c, pl.ds(2 * RB + HR, HR)], land.at[k, c, pl.ds(3 * RB + HR, HR)],
                ag2_s.at[k, 1, c], ag2_r.at[k, 1, c], left,
            ),
        )

    def scatter_one(c):
        p = c % SLOTS
        return (
            ring(part.at[p, 3, pl.ds(0, HR)], transit.at[0, c], rs1_s.at[0, c], rs1_r.at[0, c], right),
            ring(part.at[p, 3, pl.ds(HR, HR)], transit.at[1, c], rs1_s.at[1, c], rs1_r.at[1, c], left),
        )

    def scatter_two(c):
        p = c % SLOTS
        return (
            ring(part.at[p, 2], full.at[0, c], rs2_s.at[0, c], rs2_r.at[0, c], right),
            ring(part.at[p, 1], full.at[1, c], rs2_s.at[1, c], rs2_r.at[1, c], left),
        )

    def gate_copies(c):
        return [
            ring(gpart.at[c], grecv.at[j, c], gt_s.at[j, c], gt_r.at[j, c], peer)
            for j, peer in enumerate((right, left, across))
        ]

    def step_gather_one(c):
        for k in range(2):
            whole = land.at[k, c, pl.ds(0, RB)]
            pltpu.make_async_copy(whole, whole, a2a_r.at[k, c]).wait()
            for copy in gather_one(k, c):
                copy.start()

    def step_gather_two(c):
        for k in range(2):
            firsts, seconds = gather_one(k, c), gather_two(k, c)
            for first, second in zip(firsts, seconds):
                first.wait_recv()
                second.start()

    def step_compute(c):
        p = c % SLOTS
        for k in range(2):
            for copy in gather_two(k, c):
                copy.wait_recv()
                copy.wait_send()
            for copy in gather_one(k, c):
                copy.wait_send()
        for k in range(2):
            arrived = eland.at[k, c]
            pltpu.make_async_copy(arrived, arrived, ea2a_r.at[k, c]).wait()
            land[k, c] = jnp.dot(perm[0], land[k, c], preferred_element_type=F32).astype(BF16)
            eland[k, c] = jnp.dot(eperm[...], eland[k, c], preferred_element_type=F32).astype(BF16)

        def project(k, w):
            total = jnp.dot(eland[k, c], wtr[w, MAIN:, :], preferred_element_type=F32)
            for q in range(NQ):
                rows = land[k, c, q * 64 : (q + 1) * 64, :]
                total = total + jnp.dot(rows, wtr[w, q * MW : (q + 1) * MW, :], preferred_element_type=F32)
            return total

        gate_pre, up_pre, weighted = project(0, 0), project(0, 1), project(1, 2)
        logistic = jax.nn.sigmoid(gate_pre)
        activated = gate_pre * logistic
        hidden = (activated * up_pre).astype(BF16)
        pre_grad = (weighted * up_pre * logistic * (1.0 + gate_pre * (1.0 - logistic))).astype(BF16)
        up_grad = (weighted * activated).astype(BF16)
        gate_sum = jnp.sum(hidden.astype(F32) * weighted, axis=1, keepdims=True)
        gate_sum = jnp.broadcast_to(jnp.concatenate([gate_sum, gate_sum], axis=0), (128, 128))
        gpart[c] = gate_sum.T[:8, :]
        rows = pl.ds(pl.multiple_of(c * 64, 64), 64)
        acts[0, rows, :] = pre_grad
        acts[1, rows, :] = up_grad
        acts[2, rows, :] = hidden
        for copy in gate_copies(c):
            copy.start()
        parts = []
        for q in range(NQ):
            both = jnp.dot(pre_grad, wnat[0, :, q * QW : (q + 1) * QW], preferred_element_type=F32)
            both = both + jnp.dot(up_grad, wnat[1, :, q * QW : (q + 1) * QW], preferred_element_type=F32)
            parts.append(both.astype(BF16))
        message = jnp.dot(perm[1], jnp.concatenate(parts, axis=0), preferred_element_type=F32).astype(BF16)
        for rel in range(4):
            part[p, rel] = message[rel * RB : (rel + 1) * RB]
        for copy in scatter_one(c):
            copy.start()

    def step_scatter_two(c):
        p = c % SLOTS
        ones, twos = scatter_one(c), scatter_two(c)
        for j, (rel, rows) in enumerate(((2, pl.ds(0, HR)), (1, pl.ds(HR, HR)))):
            ones[j].wait_recv()
            total = part[p, rel, rows, :].astype(F32) + transit[j, c].astype(F32)
            part[p, rel, rows, :] = total.astype(BF16)
            twos[j].start()

    gr = lax.broadcasted_iota(jnp.int32, (RB, 128), 0)
    gl = lax.broadcasted_iota(jnp.int32, (RB, 128), 1)
    slot_lane = (gr >> 4) * CAP + (gr & 3)

    def ret_copy(c, m):
        rows = pl.ds(pl.multiple_of(m * 16, 16), 16)
        return pltpu.make_async_remote_copy(
            src_ref=ret.at[c, rows],
            dst_ref=back.at[c, rows],
            send_sem=ret_s.at[c],
            recv_sem=ret_r.at[c],
            device_id=(rep, partner(c, m, -1)),
            device_id_type=MESH,
        )

    def step_return(c):
        p = c % SLOTS
        for copy in scatter_two(c):
            copy.wait_recv()
            copy.wait_send()
        for copy in scatter_one(c):
            copy.wait_send()
        for copy in gate_copies(c):
            copy.wait()
        total = part[p, 0].astype(F32) + full[0, c].astype(F32) + full[1, c].astype(F32)
        ret[c, :, :QW] = total.astype(BF16)
        gate = jnp.where(gl == slot_lane, gpart[c, :1, :], 0.0)
        gate = gate + jnp.where(gl == slot_lane + 2 * NM * CAP, grecv[0, c, :1, :], 0.0)
        gate = gate + jnp.where(gl == slot_lane + NM * CAP, grecv[1, c, :1, :], 0.0)
        gate = gate + jnp.where(gl == slot_lane + 3 * NM * CAP, grecv[2, c, :1, :], 0.0)
        gate = jnp.sum(gate, axis=1, keepdims=True)
        ret[c, :, QW:] = jnp.broadcast_to(gate, (RB, 128)).astype(BF16)

        @pl.when(c == 0)
        def _():
            pltpu.make_async_copy(ret.at[0, pl.ds(0, 16)], back.at[0, pl.ds(0, 16)], ret_r.at[0]).start()

        def one(m, carry):
            ret_copy(c, m).start()
            return carry

        lax.fori_loop(jnp.where(c == 0, 1, 0), NM, one, 0)

    def grad_tile(x, cot, at, wide):
        out = pl.ds(pl.multiple_of(at, 128), wide)
        dout[0, :, out] = jnp.dot(acts_t[0], x, preferred_element_type=F32).astype(BF16)
        dout[1, :, out] = jnp.dot(acts_t[1], x, preferred_element_type=F32).astype(BF16)
        dout[2, :, out] = jnp.dot(acts_t[2], cot, preferred_element_type=F32).astype(BF16)

    def weight_grads(q, carry):
        rows = pl.ds(pl.multiple_of(q * 64, 64), 64)
        for at in range(0, MW, 256):
            wide = min(256, MW - at)
            x, cot = (land[k, :, rows, at : at + wide].reshape(NC * 64, wide) for k in range(2))
            grad_tile(x, cot, q * MW + at, wide)
        return carry

    def weight_grads_extra():
        for at in range(0, EW, 256):
            x, cot = (eland[k, :, :, at : at + 256].reshape(NC * 64, 256) for k in range(2))
            grad_tile(x, cot, MAIN + at, 256)

    def turn_acts():
        for k in range(3):
            acts_t[k] = acts[k].T

    def step(t, carry):
        pl.when(t < NC)(lambda: step_gather_one(t))
        pl.when((t >= 1) & (t < NC + 1))(lambda: step_gather_two(t - 1))
        pl.when(t == 1)(pack_extra)
        main_first, main_last = pick(t, (2, 6, 9, 12)), pick(t, (6, 9, 12, 16))
        extra_first, extra_last = pick(t, (0, 0, 4, 9)), pick(t, (0, 4, 9, 16))
        lax.fori_loop(extra_first, extra_last, send_extra, 0)
        lax.fori_loop(main_first, main_last, send_chunk, 0)
        pl.when(t == 1)(turn_weights)
        pl.when((t >= 2) & (t < NC + 2))(lambda: step_compute(t - 2))
        pl.when((t >= 3) & (t < NC + 3))(lambda: step_scatter_two(t - 3))
        pl.when((t >= 4) & (t < NC + 4))(lambda: step_return(t - 4))
        pl.when(t == NC + 1)(turn_acts)
        first = jnp.where(t == NC + 1, 0, jnp.where(t == NC + 2, 1, 3))
        last = jnp.where(t == NC + 1, 1, jnp.where(t == NC + 2, 3, jnp.where(t == NC + 3, 4, 0)))
        lax.fori_loop(first, last, weight_grads, 0)
        pl.when(t == NC + 3)(weight_grads_extra)
        return carry

    lax.fori_loop(0, NC + 4, step, 0)

    stores = [
        pltpu.make_async_copy(dout.at[k], dst.at[0], o_sem.at[k])
        for k, dst in enumerate((dg_ref, du_ref, dd_ref))
    ]
    for store in stores:
        store.start()
    skip = pl.ds(16, RB - 16)
    for c in range(NC):
        pltpu.make_async_copy(back.at[c], back.at[c], ret_r.at[c]).wait()
        rows = skip if c == 0 else pl.ds(0, RB)
        for k in range(2):
            pltpu.make_async_copy(pack.at[k, c, rows], pack.at[k, c, rows], a2a_s.at[k, c]).wait()
            pltpu.make_async_copy(epack.at[k, c, rows], epack.at[k, c, rows], ea2a_s.at[k, c]).wait()
        pltpu.make_async_copy(ret.at[c, rows], ret.at[c, rows], ret_s.at[c]).wait()
    for k in range(2):
        for copy in raw_one(k) + raw_two(k):
            copy.wait_send()
    for copy in pos_copies:
        copy.wait_send()
    for store in stores:
        store.wait()


def finish(
    back_hbm, ids_ref, g_ref, dg_ref, du_ref, dd_ref,
    tgrad_ref, ggrad_ref, og_ref, ou_ref, od_ref,
    back, grads, b_sem, in_sem, out_sem,
):
    ep = lax.axis_index("ep")
    load = pltpu.make_async_copy(back_hbm, back, b_sem)
    load.start()
    fetches = [
        pltpu.make_async_copy(src.at[0], grads.at[k], in_sem.at[k]) for k, src in enumerate((dg_ref, du_ref, dd_ref))
    ]
    stores = [
        pltpu.make_async_copy(grads.at[k], dst.at[0], out_sem.at[k]) for k, dst in enumerate((og_ref, ou_ref, od_ref))
    ]
    for fetch in fetches:
        fetch.start()
    pos = positions(ids_ref, ep // 16, (ep // 2) % 8, ep % 2)
    pos_col = jnp.broadcast_to(pos.astype(F32), (128, 128)).T[:, :1].astype(jnp.int32)
    mr = lax.broadcasted_iota(jnp.int32, (128, NC * RB), 1)
    hit = (mr >> 4) * CAP + (mr & 3) == pos_col
    load.wait()
    for q in range(NQ):
        take = jnp.where(hit & (((mr >> 2) & 3) == q), 1.0, 0.0).astype(BF16)
        rows = back[:, :, :QW].reshape(NC * RB, QW)
        tgrad_ref[:, q * QW : (q + 1) * QW] = jnp.dot(take, rows, preferred_element_type=F32).astype(BF16)
        if q == 0:
            gate = jnp.dot(take, back[:, :, QW:].reshape(NC * RB, 128), preferred_element_type=F32)
            ggrad_ref[...] = (gate.T[:1, :] / g_ref[...].astype(F32)).astype(BF16)
        if q < 3:
            fetches[q].wait()
            stores[q].start()
    for store in stores:
        store.wait()


def shards(tokens, cotangent, expert_ids, gates, gate_weight, up_weight, down_weight):
    rows, width = tokens.shape
    vmem, hbm = pl.BlockSpec(memory_space=pltpu.VMEM), pl.BlockSpec(memory_space=pl.ANY)
    dma = pltpu.SemaphoreType.DMA
    ids, gates = expert_ids.reshape(1, rows), gates.reshape(1, rows)
    weight_shape = jax.ShapeDtypeStruct((1, HID, width), BF16)
    back, *grads = pl.pallas_call(
        kernel,
        out_shape=(jax.ShapeDtypeStruct((NC, RB, BW), BF16),) + (weight_shape,) * 3,
        in_specs=[vmem] * 4 + [hbm] * 3,
        out_specs=(hbm,) * 4,
        scratch_shapes=[
            pltpu.VMEM((2, NC, 4 * RB, MW), BF16),
            pltpu.VMEM((2, NC, RB, MW), BF16),
            pltpu.VMEM((2, NQ * 128, MW), BF16),
            pltpu.VMEM((2, NC, RB, EW), BF16),
            pltpu.VMEM((2, NC, RB, EW), BF16),
            pltpu.VMEM((2, 4 * 128, EW), BF16),
            pltpu.VMEM((8, 128), F32),
            pltpu.VMEM((3, 8, 128), F32),
            pltpu.VMEM((2, 256, 256), BF16),
            pltpu.VMEM((64, 64), BF16),
            pltpu.VMEM((3, HID, width), BF16),
            pltpu.VMEM((3, width, HID), BF16),
            pltpu.VMEM((SLOTS, 4, RB, QW), BF16),
            pltpu.VMEM((2, NC, HR, QW), BF16),
            pltpu.VMEM((2, NC, RB, QW), BF16),
            pltpu.VMEM((NC, 8, 128), F32),
            pltpu.VMEM((3, NC, 8, 128), F32),
            pltpu.VMEM((NC, RB, BW), BF16),
            pltpu.VMEM((3, NC * 64, HID), BF16),
            pltpu.VMEM((3, HID, NC * 64), BF16),
            pltpu.VMEM((3, HID, width), BF16),
            dma((2, NC)), dma((2, NC)), dma((2, NC)), dma((2, NC)),
            dma((2, 2)), dma((2, 2)), dma((2, 2)), dma((2, 2)), dma((3,)), dma((3,)),
            dma((2, 2, NC)), dma((2, 2, NC)), dma((2, 2, NC)), dma((2, 2, NC)),
            dma((2, NC)), dma((2, NC)), dma((2, NC)), dma((2, NC)),
            dma((3, NC)), dma((3, NC)),
            dma((NC,)), dma((NC,)),
            dma((3,)), dma((3,)),
        ],
        compiler_params=pltpu.CompilerParams(
            collective_id=0, has_side_effects=True, vmem_limit_bytes=62 * 1024 * 1024
        ),
    )(
        tokens,
        cotangent,
        ids,
        gates,
        jnp.transpose(gate_weight, (0, 2, 1)),
        jnp.transpose(up_weight, (0, 2, 1)),
        down_weight,
    )
    token_grad, gates_grad, gate_grad, upper_grad, down_grad = pl.pallas_call(
        finish,
        out_shape=(
            jax.ShapeDtypeStruct((rows, width), BF16),
            jax.ShapeDtypeStruct((1, rows), BF16),
        ) + (weight_shape,) * 3,
        in_specs=[hbm, vmem, vmem] + [hbm] * 3,
        out_specs=(vmem, vmem, hbm, hbm, hbm),
        scratch_shapes=[
            pltpu.VMEM((NC, RB, BW), BF16), pltpu.VMEM((3, HID, width), BF16), dma, dma((3,)), dma((3,)),
        ],
        compiler_params=pltpu.CompilerParams(vmem_limit_bytes=62 * 1024 * 1024),
    )(back, ids, gates, *grads)
    return (
        token_grad,
        gates_grad.reshape(rows, 1),
        jnp.transpose(gate_grad, (0, 2, 1)),
        jnp.transpose(upper_grad, (0, 2, 1)),
        down_grad,
    )


def solution(mesh):
    in_specs = (
        P(("rep", "ep"), None),
        P(("rep", "ep"), None),
        P(("rep", "ep"), None),
        P(("rep", "ep"), None),
        P("ep", None, "rep"),
        P("ep", None, "rep"),
        P("ep", "rep", None),
    )
    out_specs = (
        P(("rep", "ep"), None),
        P(("rep", "ep"), None),
        P("ep", None, "rep"),
        P("ep", None, "rep"),
        P("ep", "rep", None),
    )
    return jax.shard_map(shards, mesh=mesh, in_specs=in_specs, out_specs=out_specs, check_vma=False)
```

```python
import jax
import jax.numpy as jnp
from jax import lax
from jax.experimental import pallas as pl
from jax.experimental.pallas import tpu as pltpu
from jax.sharding import PartitionSpec as P

MESH = pl.DeviceIdType.MESH
F32, BF16 = jnp.float32, jnp.bfloat16

DZ = (0, 7, 2, 5, 3, 4, 6, 1)
NC = 16
NM = 4
CAP = 4
NQ = 4
RB = NM * NQ * CAP
HR = RB // 2
QW = 1024
HW = 512
EW = 512
MW = QW - EW // NQ
MAIN = NQ * MW
BW = QW + 128
HID = 192
SLOTS = 3
ROWS = NC * NM * CAP


def pick(index, table):
    return sum(jnp.where(index == k, v, 0) for k, v in enumerate(table) if v)


def positions(ids_ref, my_y, my_z, my_c):
    ids = ids_ref[...].astype(F32)
    by_lane = jnp.broadcast_to(ids, (128, 128))
    by_row = by_lane.T
    a = lax.broadcasted_iota(jnp.int32, (128, 128), 0)
    b = lax.broadcasted_iota(jnp.int32, (128, 128), 1)
    same = jnp.where(by_lane == by_row, 1, 0)
    rank = jnp.sum(jnp.where(a < b, same, 0), axis=0, keepdims=True)
    expert = ids_ref[...]
    dy = ((expert >> 4) - my_y) & 3
    dz = (((expert >> 1) & 7) - my_z) & 7
    dc = (expert - my_c) & 1
    at_z = sum(jnp.where(dz == d, k, 0) for k, d in enumerate(DZ) if k)
    return ((at_z * 2 + dc) * NM + dy) * CAP + rank


def kernel(
    tok_ref, cot_ref, ids_ref, g_ref, wg_ref, wu_ref, wd_ref,
    back, dg_ref, du_ref, dd_ref,
    land, pack, stack, eland, epack, estack, pos_own, pos_recv, perm, eperm, wnat, wtr, wpair, pre_own, pre_pair, part, first, second, gpart, grecv, ret, acts, acts_t, dout,
    a2a_s, a2a_r, ea2a_s, ea2a_r, raw1_s, raw1_r, raw2_s, raw2_r, pos_s, pos_r, ag1_s, ag1_r, ag2_s, ag2_r, rs1_s, rs1_r, rs2_s, rs2_r, pre_s, pre_r, wx_s, wx_r, gt_s, gt_r, ret_s, ret_r, w_sem, o_sem,
):
    rep, ep = lax.axis_index("rep"), lax.axis_index("ep")
    my_y, my_z, my_c = ep // 16, (ep // 2) % 8, ep % 2
    side = 1 - 2 * ((rep + my_c) % 2)
    pair, other, across = (rep + side + 4) % 4, (rep - side + 4) % 4, (rep + 2) % 4
    half = ((rep + 1 - my_c) // 2) % 2
    mine, theirs = (pl.ds(pl.multiple_of(h * 2048, 2048), 2048) for h in (half, 1 - half))

    loads = [
        pltpu.make_async_copy(src.at[0], wnat.at[k], w_sem.at[k])
        for k, src in enumerate((wg_ref, wu_ref, wd_ref))
    ]
    for load in loads:
        load.start()

    barrier = pltpu.get_barrier_semaphore()

    def greet(k, carry):
        pl.semaphore_signal(barrier, inc=1, device_id=(rep, (ep + k) % 64), device_id_type=MESH)
        return carry

    lax.fori_loop(1, 64, greet, 0)
    for peer in (pair, other, across):
        pl.semaphore_signal(barrier, inc=1, device_id=(peer, ep), device_id_type=MESH)

    pos = positions(ids_ref, my_y, my_z, my_c)
    gates_row = g_ref[...].astype(F32)
    gates_col = jnp.broadcast_to(gates_row, (128, 128)).T[:, :1]
    pos_own[...] = jnp.broadcast_to(pos.astype(F32), (8, 128))
    for q in range(NQ):
        stack[0, q * 128 : (q + 1) * 128, :] = tok_ref[:, q * MW : (q + 1) * MW]
        cot = cot_ref[:, q * MW : (q + 1) * MW].astype(F32)
        stack[1, q * 128 : (q + 1) * 128, :] = (cot * gates_col).astype(BF16)
    estack[0, :128, :] = tok_ref[:, MAIN:]
    estack[1, :128, :] = (cot_ref[:, MAIN:].astype(F32) * gates_col).astype(BF16)

    pr = lax.broadcasted_iota(jnp.int32, (256, 256), 0)
    pc = lax.broadcasted_iota(jnp.int32, (256, 256), 1)
    perm[0] = jnp.where(pc == ((pr & 63) >> 2) * 16 + (pr >> 6) * 4 + (pr & 3), 1.0, 0.0).astype(BF16)
    perm[1] = jnp.where(pr == ((pc & 63) >> 2) * 16 + (pc >> 6) * 4 + (pc & 3), 1.0, 0.0).astype(BF16)

    er = lax.broadcasted_iota(jnp.int32, (64, 64), 0)
    ec = lax.broadcasted_iota(jnp.int32, (64, 64), 1)
    eperm[...] = jnp.where(ec == ((er & 15) >> 2) * 16 + (er >> 4) * 4 + (er & 3), 1.0, 0.0).astype(BF16)

    def partner(c, m, sign):
        z = (my_z + sign * pick(c // 2, DZ) + 8) % 8
        y = (my_y + sign * m + 4) % 4
        return y * 16 + z * 2 + (my_c + c) % 2

    sr = lax.broadcasted_iota(jnp.int32, (2 * RB, 512), 0)
    sc = lax.broadcasted_iota(jnp.int32, (2 * RB, 512), 1)
    slot_of_row = (sr >> 4) * CAP + (sr & 3)
    quarter = (sr >> 2) & 3
    quarter_ok = quarter == (sc >> 7)
    changed = (sr >= RB) & ((quarter == 1) | (quarter == 2))
    block_ok = jnp.where(changed, 3 - quarter, quarter) == (sc >> 7)
    pos4 = jnp.concatenate([pos] * NQ, axis=1)

    def fill_from(source, target, ok, places, j):
        onehot = jnp.where(ok & (places - j * (2 * NM * CAP) == slot_of_row), 1.0, 0.0).astype(BF16)
        for k in range(2):
            rows = jnp.dot(onehot, source[k], preferred_element_type=F32).astype(BF16)
            target[k, 2 * j] = rows[:RB]
            target[k, 2 * j + 1] = rows[RB:]

    def fill(j, carry):
        fill_from(stack, pack, quarter_ok, pos4, j)
        return carry

    lax.fori_loop(0, NC // 2, fill, 0)

    def send_from(source, target, send_sem, recv_sem, c):
        def one(m, inner):
            rows = pl.ds(pl.multiple_of(m * 16, 16), 16)
            for k in range(2):
                pltpu.make_async_remote_copy(
                    src_ref=source.at[k, c, rows],
                    dst_ref=target.at[k, c, rows],
                    send_sem=send_sem.at[k, c],
                    recv_sem=recv_sem.at[k, c],
                    device_id=(rep, partner(c, m, 1)),
                    device_id_type=MESH,
                ).start()
            return inner

        lax.fori_loop(jnp.where(c == 0, 1, 0), NM, one, 0)

    def send_chunk(c, carry):
        send_from(pack, land, a2a_s, a2a_r, c)
        return carry

    def send_extra(c, carry):
        send_from(epack, eland, ea2a_s, ea2a_r, c)
        return carry

    def ring(src, dst, send_sem, recv_sem, peer):
        return pltpu.make_async_remote_copy(
            src_ref=src, dst_ref=dst, send_sem=send_sem, recv_sem=recv_sem,
            device_id=(peer, ep), device_id_type=MESH,
        )

    def raw_one(k):
        own = estack.at[k, pl.ds(0, 128)]
        return (
            ring(own, estack.at[k, pl.ds(128, 128)], raw1_s.at[k, 0], raw1_r.at[k, 0], pair),
            ring(own, estack.at[k, pl.ds(256, 128)], raw1_s.at[k, 1], raw1_r.at[k, 1], other),
        )

    def raw_two(k):
        return (
            ring(
                estack.at[k, pl.ds(128, 64)], estack.at[k, pl.ds(384, 64)],
                raw2_s.at[k, 0], raw2_r.at[k, 0], other,
            ),
            ring(
                estack.at[k, pl.ds(320, 64)], estack.at[k, pl.ds(448, 64)],
                raw2_s.at[k, 1], raw2_r.at[k, 1], pair,
            ),
        )

    pos_copies = [
        ring(pos_own, pos_recv.at[j], pos_s.at[j], pos_r.at[j], peer) for j, peer in enumerate((pair, other, across))
    ]
    weight_copies = [
        ring(wnat.at[k, :, theirs], wpair.at[pl.ds(k * HID, HID)], wx_s.at[k], wx_r.at[k], pair) for k in range(2)
    ]

    pl.semaphore_wait(barrier, 66)
    for copy in pos_copies:
        copy.start()
    for k in range(2):
        for copy in raw_one(k):
            copy.start()
    for k in range(2):
        pltpu.make_async_copy(pack.at[k, 0, pl.ds(0, 16)], land.at[k, 0, pl.ds(0, 16)], a2a_r.at[k, 0]).start()
    lax.fori_loop(0, 2, send_chunk, 0)
    for k in range(2):
        for one, two in zip(raw_one(k), raw_two(k)):
            one.wait_recv()
            two.start()
    for load in loads:
        load.wait()

    def pack_extra():
        for k in range(2):
            for copy in raw_two(k):
                copy.wait_recv()
        for copy in pos_copies:
            copy.wait_recv()
        places = jnp.concatenate([pos_own[:1, :]] + [pos_recv[j, :1, :] for j in range(3)], axis=1).astype(jnp.int32)

        def one(j, carry):
            fill_from(estack, epack, block_ok, places, j)
            return carry

        lax.fori_loop(0, NC // 2, one, 0)
        for k in range(2):
            pltpu.make_async_copy(
                epack.at[k, 0, pl.ds(0, 16)], eland.at[k, 0, pl.ds(0, 16)], ea2a_r.at[k, 0]
            ).start()

    def turn_weights():
        def turn(j, carry):
            cols = pl.ds(pl.multiple_of(j * 512, 512), 512)
            for k in range(3):
                wtr[k, cols, :] = wnat[k, :, cols].T
            return carry

        lax.fori_loop(0, 8, turn, 0)

    def gather_one(k, c):
        own = land.at[k, c, pl.ds(0, RB)]
        return (
            ring(own, land.at[k, c, pl.ds(RB, RB)], ag1_s.at[k, 0, c], ag1_r.at[k, 0, c], pair),
            ring(own, land.at[k, c, pl.ds(2 * RB, RB)], ag1_s.at[k, 1, c], ag1_r.at[k, 1, c], other),
        )

    def gather_two(k, c):
        return (
            ring(
                land.at[k, c, pl.ds(RB, HR)], land.at[k, c, pl.ds(3 * RB, HR)],
                ag2_s.at[k, 0, c], ag2_r.at[k, 0, c], other,
            ),
            ring(
                land.at[k, c, pl.ds(2 * RB + HR, HR)], land.at[k, c, pl.ds(3 * RB + HR, HR)],
                ag2_s.at[k, 1, c], ag2_r.at[k, 1, c], pair,
            ),
        )

    def pre_copy(c):
        return ring(pre_own.at[c], pre_pair.at[c], pre_s.at[c], pre_r.at[c], pair)

    def scatter_one(c):
        return ring(part.at[c % SLOTS, pl.ds(2 * RB, 2 * RB)], first.at[c], rs1_s.at[c], rs1_r.at[c], other)

    def scatter_two(c):
        return ring(part.at[c % SLOTS, pl.ds(RB, RB)], second.at[c], rs2_s.at[c], rs2_r.at[c], pair)

    def gate_copies(c):
        return [
            ring(gpart.at[c], grecv.at[j, c], gt_s.at[j, c], gt_r.at[j, c], peer)
            for j, peer in enumerate((pair, other, across))
        ]

    def step_gather_one(c):
        for k in range(2):
            whole = land.at[k, c, pl.ds(0, RB)]
            pltpu.make_async_copy(whole, whole, a2a_r.at[k, c]).wait()
            for copy in gather_one(k, c):
                copy.start()

    def step_gather_two(c):
        for k in range(2):
            for one, two in zip(gather_one(k, c), gather_two(k, c)):
                one.wait_recv()
                two.start()

    def step_compute(c):
        for k in range(2):
            for copy in gather_two(k, c):
                copy.wait_recv()
                copy.wait_send()
            for copy in gather_one(k, c):
                copy.wait_send()
        for k in range(2):
            arrived = eland.at[k, c]
            pltpu.make_async_copy(arrived, arrived, ea2a_r.at[k, c]).wait()
            land[k, c] = jnp.dot(perm[0], land[k, c], preferred_element_type=F32).astype(BF16)
            eland[k, c] = jnp.dot(eperm[...], eland[k, c], preferred_element_type=F32).astype(BF16)

        def project(k, w):
            total = jnp.dot(eland[k, c], wtr[w, MAIN:, :], preferred_element_type=F32)
            for q in range(NQ):
                rows = land[k, c, q * 64 : (q + 1) * 64, :]
                total = total + jnp.dot(rows, wtr[w, q * MW : (q + 1) * MW, :], preferred_element_type=F32)
            return total

        gate_pre, up_pre, weighted = project(0, 0), project(0, 1), project(1, 2)
        logistic = jax.nn.sigmoid(gate_pre)
        activated = gate_pre * logistic
        hidden = (activated * up_pre).astype(BF16)
        pre_grad = (weighted * up_pre * logistic * (1.0 + gate_pre * (1.0 - logistic))).astype(BF16)
        up_grad = (weighted * activated).astype(BF16)
        gate_sum = jnp.sum(hidden.astype(F32) * weighted, axis=1, keepdims=True)
        gate_sum = jnp.broadcast_to(jnp.concatenate([gate_sum, gate_sum], axis=0), (128, 128))
        gpart[c] = gate_sum.T[:1, :]
        rows = pl.ds(pl.multiple_of(c * 64, 64), 64)
        acts[0, rows, :] = pre_grad
        acts[1, rows, :] = up_grad
        acts[2, rows, :] = hidden
        pre_own[c] = jnp.concatenate([pre_grad, up_grad], axis=1)
        pre_copy(c).start()
        for copy in gate_copies(c):
            copy.start()

    def step_scatter_one(c):
        rows = pl.ds(pl.multiple_of(c * 64, 64), 64)
        total = jnp.dot(acts[0, rows, :], wnat[0, :, mine], preferred_element_type=F32)
        total = total + jnp.dot(acts[1, rows, :], wnat[1, :, mine], preferred_element_type=F32)
        pl.when(c == 0)(lambda: [copy.wait_recv() for copy in weight_copies] and None)
        pre_copy(c).wait()
        swapped = jnp.concatenate([pre_pair[c, b * 16 : (b + 1) * 16, :] for b in (1, 0, 3, 2)], axis=0)
        total = total + jnp.dot(swapped, wpair[...], preferred_element_type=F32)
        total = total.astype(BF16)
        stacked = jnp.concatenate([total[:, q * HW : (q + 1) * HW] for q in range(NQ)], axis=0)
        part[c % SLOTS] = jnp.dot(perm[1], stacked, preferred_element_type=F32).astype(BF16)
        scatter_one(c).start()

    def step_scatter_two(c):
        p = c % SLOTS
        scatter_one(c).wait_recv()
        total = part[p, RB : 2 * RB, :].astype(F32) + first[c, RB:, :].astype(F32)
        part[p, RB : 2 * RB, :] = total.astype(BF16)
        scatter_two(c).start()

    gr = lax.broadcasted_iota(jnp.int32, (RB, 128), 0)
    gl = lax.broadcasted_iota(jnp.int32, (RB, 128), 1)
    slot_lane = (gr >> 4) * CAP + (gr & 3)

    def ret_copy(c, m):
        rows = pl.ds(pl.multiple_of(m * 16, 16), 16)
        return pltpu.make_async_remote_copy(
            src_ref=ret.at[c, rows],
            dst_ref=back.at[c, rows],
            send_sem=ret_s.at[c],
            recv_sem=ret_r.at[c],
            device_id=(rep, partner(c, m, -1)),
            device_id_type=MESH,
        )

    def step_return(c):
        p = c % SLOTS
        scatter_two(c).wait()
        scatter_one(c).wait_send()
        for copy in gate_copies(c):
            copy.wait()
        total = part[p, :RB, :].astype(F32) + first[c, :RB, :].astype(F32)
        ret[c, :, pl.ds(pl.multiple_of(half * HW, HW), HW)] = total.astype(BF16)
        ret[c, :, pl.ds(pl.multiple_of((1 - half) * HW, HW), HW)] = second[c]
        gate = jnp.where(gl == slot_lane, gpart[c], 0.0)
        gate = gate + jnp.where(gl == slot_lane + NM * CAP, grecv[0, c], 0.0)
        gate = gate + jnp.where(gl == slot_lane + 2 * NM * CAP, grecv[1, c], 0.0)
        gate = gate + jnp.where(gl == slot_lane + 3 * NM * CAP, grecv[2, c], 0.0)
        gate = jnp.sum(gate, axis=1, keepdims=True)
        ret[c, :, QW:] = jnp.broadcast_to(gate, (RB, 128)).astype(BF16)

        @pl.when(c == 0)
        def _():
            pltpu.make_async_copy(ret.at[0, pl.ds(0, 16)], back.at[0, pl.ds(0, 16)], ret_r.at[0]).start()

        def one(m, carry):
            ret_copy(c, m).start()
            return carry

        lax.fori_loop(jnp.where(c == 0, 1, 0), NM, one, 0)

    def grad_tile(x, cot, at, wide):
        out = pl.ds(pl.multiple_of(at, 128), wide)
        dout[0, :, out] = jnp.dot(acts_t[0], x, preferred_element_type=F32).astype(BF16)
        dout[1, :, out] = jnp.dot(acts_t[1], x, preferred_element_type=F32).astype(BF16)
        dout[2, :, out] = jnp.dot(acts_t[2], cot, preferred_element_type=F32).astype(BF16)

    def weight_grads(q, carry):
        rows = pl.ds(pl.multiple_of(q * 64, 64), 64)
        for at in range(0, MW, 256):
            wide = min(256, MW - at)
            x, cot = (land[k, :, rows, at : at + wide].reshape(NC * 64, wide) for k in range(2))
            grad_tile(x, cot, q * MW + at, wide)
        return carry

    def weight_grads_extra():
        for at in range(0, EW, 256):
            x, cot = (eland[k, :, :, at : at + 256].reshape(NC * 64, 256) for k in range(2))
            grad_tile(x, cot, MAIN + at, 256)

    def turn_acts():
        for k in range(3):
            acts_t[k] = acts[k].T

    def step(t, carry):
        pl.when(t < NC)(lambda: step_gather_one(t))
        pl.when((t >= 1) & (t < NC + 1))(lambda: step_gather_two(t - 1))
        pl.when(t == 1)(pack_extra)
        main_first, main_last = pick(t, (2, 6, 9, 12)), pick(t, (6, 9, 12, 16))
        extra_first, extra_last = pick(t, (0, 0, 4, 9)), pick(t, (0, 4, 9, 16))
        lax.fori_loop(extra_first, extra_last, send_extra, 0)
        lax.fori_loop(main_first, main_last, send_chunk, 0)
        pl.when(t == 1)(turn_weights)
        pl.when(t == 1)(lambda: [copy.start() for copy in weight_copies] and None)
        pl.when((t >= 2) & (t < NC + 2))(lambda: step_compute(t - 2))
        pl.when((t >= 3) & (t < NC + 3))(lambda: step_scatter_one(t - 3))
        pl.when((t >= 4) & (t < NC + 4))(lambda: step_scatter_two(t - 4))
        pl.when((t >= 5) & (t < NC + 5))(lambda: step_return(t - 5))
        pl.when(t == NC + 1)(turn_acts)
        u = t - NC
        lax.fori_loop(pick(u, (0, 0, 1, 2)), pick(u, (0, 1, 2, 4)), weight_grads, 0)
        pl.when(t == NC + 4)(weight_grads_extra)
        return carry

    lax.fori_loop(0, NC + 5, step, 0)

    stores = [
        pltpu.make_async_copy(dout.at[k], dst.at[0], o_sem.at[k])
        for k, dst in enumerate((dg_ref, du_ref, dd_ref))
    ]
    for store in stores:
        store.start()
    skip = pl.ds(16, RB - 16)
    for c in range(NC):
        pltpu.make_async_copy(back.at[c], back.at[c], ret_r.at[c]).wait()
        rows = skip if c == 0 else pl.ds(0, RB)
        for k in range(2):
            pltpu.make_async_copy(pack.at[k, c, rows], pack.at[k, c, rows], a2a_s.at[k, c]).wait()
            pltpu.make_async_copy(epack.at[k, c, rows], epack.at[k, c, rows], ea2a_s.at[k, c]).wait()
        pltpu.make_async_copy(ret.at[c, rows], ret.at[c, rows], ret_s.at[c]).wait()
    for k in range(2):
        for copy in raw_one(k) + raw_two(k):
            copy.wait_send()
    for copy in pos_copies + weight_copies:
        copy.wait_send()
    for store in stores:
        store.wait()


def finish(
    back_hbm, ids_ref, g_ref, dg_ref, du_ref, dd_ref,
    tgrad_ref, ggrad_ref, og_ref, ou_ref, od_ref,
    back, grads, b_sem, in_sem, out_sem,
):
    ep = lax.axis_index("ep")
    load = pltpu.make_async_copy(back_hbm, back, b_sem)
    load.start()
    fetches = [
        pltpu.make_async_copy(src.at[0], grads.at[k], in_sem.at[k]) for k, src in enumerate((dg_ref, du_ref, dd_ref))
    ]
    stores = [
        pltpu.make_async_copy(grads.at[k], dst.at[0], out_sem.at[k]) for k, dst in enumerate((og_ref, ou_ref, od_ref))
    ]
    for fetch in fetches:
        fetch.start()
    pos = positions(ids_ref, ep // 16, (ep // 2) % 8, ep % 2)
    pos_col = jnp.broadcast_to(pos.astype(F32), (128, 128)).T[:, :1].astype(jnp.int32)
    mr = lax.broadcasted_iota(jnp.int32, (128, NC * RB), 1)
    hit = (mr >> 4) * CAP + (mr & 3) == pos_col
    load.wait()
    for q in range(NQ):
        take = jnp.where(hit & (((mr >> 2) & 3) == q), 1.0, 0.0).astype(BF16)
        rows = back[:, :, :QW].reshape(NC * RB, QW)
        found = jnp.dot(take, rows, preferred_element_type=F32).astype(BF16)
        for h in range(2):
            at = h * 2048 + q * HW
            tgrad_ref[:, at : at + HW] = found[:, h * HW : (h + 1) * HW]
        if q == 0:
            gate = jnp.dot(take, back[:, :, QW:].reshape(NC * RB, 128), preferred_element_type=F32)
            ggrad_ref[...] = (gate.T[:1, :] / g_ref[...].astype(F32)).astype(BF16)
        if q < 3:
            fetches[q].wait()
            stores[q].start()
    for store in stores:
        store.wait()


def shards(tokens, cotangent, expert_ids, gates, gate_weight, up_weight, down_weight):
    rows, width = tokens.shape
    vmem, hbm = pl.BlockSpec(memory_space=pltpu.VMEM), pl.BlockSpec(memory_space=pl.ANY)
    dma = pltpu.SemaphoreType.DMA
    ids, gates = expert_ids.reshape(1, rows), gates.reshape(1, rows)
    weight_shape = jax.ShapeDtypeStruct((1, HID, width), BF16)
    back, *grads = pl.pallas_call(
        kernel,
        out_shape=(jax.ShapeDtypeStruct((NC, RB, BW), BF16),) + (weight_shape,) * 3,
        in_specs=[vmem] * 4 + [hbm] * 3,
        out_specs=(hbm,) * 4,
        scratch_shapes=[
            pltpu.VMEM((2, NC, 4 * RB, MW), BF16),
            pltpu.VMEM((2, NC, RB, MW), BF16),
            pltpu.VMEM((2, NQ * 128, MW), BF16),
            pltpu.VMEM((2, NC, RB, EW), BF16),
            pltpu.VMEM((2, NC, RB, EW), BF16),
            pltpu.VMEM((2, 4 * 128, EW), BF16),
            pltpu.VMEM((8, 128), F32),
            pltpu.VMEM((3, 8, 128), F32),
            pltpu.VMEM((2, 256, 256), BF16),
            pltpu.VMEM((64, 64), BF16),
            pltpu.VMEM((3, HID, width), BF16),
            pltpu.VMEM((3, width, HID), BF16),
            pltpu.VMEM((2 * HID, width // 2), BF16),
            pltpu.VMEM((NC, 64, 2 * HID), BF16),
            pltpu.VMEM((NC, 64, 2 * HID), BF16),
            pltpu.VMEM((SLOTS, 4 * RB, HW), BF16),
            pltpu.VMEM((NC, 2 * RB, HW), BF16),
            pltpu.VMEM((NC, RB, HW), BF16),
            pltpu.VMEM((NC, 1, 128), F32),
            pltpu.VMEM((3, NC, 1, 128), F32),
            pltpu.VMEM((NC, RB, BW), BF16),
            pltpu.VMEM((3, NC * 64, HID), BF16),
            pltpu.VMEM((3, HID, NC * 64), BF16),
            pltpu.VMEM((3, HID, width), BF16),
            dma((2, NC)), dma((2, NC)), dma((2, NC)), dma((2, NC)),
            dma((2, 2)), dma((2, 2)), dma((2, 2)), dma((2, 2)), dma((3,)), dma((3,)),
            dma((2, 2, NC)), dma((2, 2, NC)), dma((2, 2, NC)), dma((2, 2, NC)),
            dma((NC,)), dma((NC,)), dma((NC,)), dma((NC,)), dma((NC,)), dma((NC,)), dma((2,)), dma((2,)),
            dma((3, NC)), dma((3, NC)),
            dma((NC,)), dma((NC,)),
            dma((3,)), dma((3,)),
        ],
        compiler_params=pltpu.CompilerParams(
            collective_id=0, has_side_effects=True, vmem_limit_bytes=62 * 1024 * 1024
        ),
    )(
        tokens,
        cotangent,
        ids,
        gates,
        jnp.transpose(gate_weight, (0, 2, 1)),
        jnp.transpose(up_weight, (0, 2, 1)),
        down_weight,
    )
    token_grad, gates_grad, gate_grad, upper_grad, down_grad = pl.pallas_call(
        finish,
        out_shape=(
            jax.ShapeDtypeStruct((rows, width), BF16),
            jax.ShapeDtypeStruct((1, rows), BF16),
        ) + (weight_shape,) * 3,
        in_specs=[hbm, vmem, vmem] + [hbm] * 3,
        out_specs=(vmem, vmem, hbm, hbm, hbm),
        scratch_shapes=[
            pltpu.VMEM((NC, RB, BW), BF16), pltpu.VMEM((3, HID, width), BF16), dma, dma((3,)), dma((3,)),
        ],
        compiler_params=pltpu.CompilerParams(vmem_limit_bytes=62 * 1024 * 1024),
    )(back, ids, gates, *grads)
    return (
        token_grad,
        gates_grad.reshape(rows, 1),
        jnp.transpose(gate_grad, (0, 2, 1)),
        jnp.transpose(upper_grad, (0, 2, 1)),
        down_grad,
    )


def solution(mesh):
    in_specs = (
        P(("rep", "ep"), None),
        P(("rep", "ep"), None),
        P(("rep", "ep"), None),
        P(("rep", "ep"), None),
        P("ep", None, "rep"),
        P("ep", None, "rep"),
        P("ep", "rep", None),
    )
    out_specs = (
        P(("rep", "ep"), None),
        P(("rep", "ep"), None),
        P("ep", None, "rep"),
        P("ep", None, "rep"),
        P("ep", "rep", None),
    )
    return jax.shard_map(shards, mesh=mesh, in_specs=in_specs, out_specs=out_specs, check_vma=False)
```

```python
import jax
import jax.numpy as jnp
from jax import lax
from jax.experimental import pallas as pl
from jax.experimental.pallas import tpu as pltpu
from jax.sharding import PartitionSpec as P

MESH = pl.DeviceIdType.MESH
F32, BF16 = jnp.float32, jnp.bfloat16

DZ = (0, 7, 2, 5, 3, 4, 6, 1)
NC = 16
NM = 4
CAP = 4
NQ = 4
RB = NM * NQ * CAP
HR = RB // 2
QW = 1024
HW = 512
EW = 512
MW = QW - EW // NQ
MAIN = NQ * MW
BW = QW + 128
HID = 192
SLOTS = 3
ROWS = NC * NM * CAP


def pick(index, table):
    return sum(jnp.where(index == k, v, 0) for k, v in enumerate(table) if v)


def positions(ids_ref, my_y, my_z, my_c):
    ids = ids_ref[...].astype(F32)
    by_lane = jnp.broadcast_to(ids, (128, 128))
    by_row = by_lane.T
    a = lax.broadcasted_iota(jnp.int32, (128, 128), 0)
    b = lax.broadcasted_iota(jnp.int32, (128, 128), 1)
    same = jnp.where(by_lane == by_row, 1, 0)
    rank = jnp.sum(jnp.where(a < b, same, 0), axis=0, keepdims=True)
    expert = ids_ref[...]
    dy = ((expert >> 4) - my_y) & 3
    dz = (((expert >> 1) & 7) - my_z) & 7
    dc = (expert - my_c) & 1
    at_z = sum(jnp.where(dz == d, k, 0) for k, d in enumerate(DZ) if k)
    return ((at_z * 2 + dc) * NM + dy) * CAP + rank


def kernel(
    tok_ref, cot_ref, ids_ref, g_ref, wg_ref, wu_ref, wd_ref,
    back, dg_ref, du_ref, dd_ref,
    land, pack, stack, eland, epack, estack, pos_own, pos_recv, perm, eperm, wnat, wtr, wpair, pre_own, pre_pair, part, first, second, gpart, grecv, ret, acts, acts_t, dout,
    a2a_s, a2a_r, ea2a_s, ea2a_r, raw1_s, raw1_r, raw2_s, raw2_r, pos_s, pos_r, ag1_s, ag1_r, ag2_s, ag2_r, rs1_s, rs1_r, rs2_s, rs2_r, pre_s, pre_r, wx_s, wx_r, gt_s, gt_r, ret_s, ret_r, w_sem, o_sem,
):
    rep, ep = lax.axis_index("rep"), lax.axis_index("ep")
    my_y, my_z, my_c = ep // 16, (ep // 2) % 8, ep % 2
    side = 1 - 2 * ((rep + my_c) % 2)
    pair, other, across = (rep + side + 4) % 4, (rep - side + 4) % 4, (rep + 2) % 4
    half = ((rep + 1 - my_c) // 2) % 2
    mine, theirs = (pl.ds(pl.multiple_of(h * 2048, 2048), 2048) for h in (half, 1 - half))

    loads = [
        pltpu.make_async_copy(src.at[0], wnat.at[k], w_sem.at[k])
        for k, src in enumerate((wg_ref, wu_ref, wd_ref))
    ]
    for load in loads:
        load.start()

    barrier = pltpu.get_barrier_semaphore()

    def greet(k, carry):
        pl.semaphore_signal(barrier, inc=1, device_id=(rep, (ep + k) % 64), device_id_type=MESH)
        return carry

    lax.fori_loop(1, 64, greet, 0)
    for peer in (pair, other, across):
        pl.semaphore_signal(barrier, inc=1, device_id=(peer, ep), device_id_type=MESH)

    pos = positions(ids_ref, my_y, my_z, my_c)
    gates_row = g_ref[...].astype(F32)
    gates_col = jnp.broadcast_to(gates_row, (128, 128)).T[:, :1]
    pos_own[...] = jnp.broadcast_to(pos.astype(F32), (8, 128))
    for q in range(NQ):
        stack[0, q * 128 : (q + 1) * 128, :] = tok_ref[:, q * MW : (q + 1) * MW]
        cot = cot_ref[:, q * MW : (q + 1) * MW].astype(F32)
        stack[1, q * 128 : (q + 1) * 128, :] = (cot * gates_col).astype(BF16)
    estack[0, :128, :] = tok_ref[:, MAIN:]
    estack[1, :128, :] = (cot_ref[:, MAIN:].astype(F32) * gates_col).astype(BF16)

    pr = lax.broadcasted_iota(jnp.int32, (256, 256), 0)
    pc = lax.broadcasted_iota(jnp.int32, (256, 256), 1)
    perm[0] = jnp.where(pc == ((pr & 63) >> 2) * 16 + (pr >> 6) * 4 + (pr & 3), 1.0, 0.0).astype(BF16)
    perm[1] = jnp.where(pr == ((pc & 63) >> 2) * 16 + (pc >> 6) * 4 + (pc & 3), 1.0, 0.0).astype(BF16)

    er = lax.broadcasted_iota(jnp.int32, (64, 64), 0)
    ec = lax.broadcasted_iota(jnp.int32, (64, 64), 1)
    eperm[...] = jnp.where(ec == ((er & 15) >> 2) * 16 + (er >> 4) * 4 + (er & 3), 1.0, 0.0).astype(BF16)

    def partner(c, m, sign):
        z = (my_z + sign * pick(c // 2, DZ) + 8) % 8
        y = (my_y + sign * m + 4) % 4
        return y * 16 + z * 2 + (my_c + c) % 2

    sr = lax.broadcasted_iota(jnp.int32, (2 * RB, 512), 0)
    sc = lax.broadcasted_iota(jnp.int32, (2 * RB, 512), 1)
    slot_of_row = (sr >> 4) * CAP + (sr & 3)
    quarter = (sr >> 2) & 3
    quarter_ok = quarter == (sc >> 7)
    changed = (sr >= RB) & ((quarter == 1) | (quarter == 2))
    block_ok = jnp.where(changed, 3 - quarter, quarter) == (sc >> 7)
    pos4 = jnp.concatenate([pos] * NQ, axis=1)

    def fill_from(source, target, ok, places, j):
        onehot = jnp.where(ok & (places - j * (2 * NM * CAP) == slot_of_row), 1.0, 0.0).astype(BF16)
        for k in range(2):
            rows = jnp.dot(onehot, source[k], preferred_element_type=F32).astype(BF16)
            target[k, 2 * j] = rows[:RB]
            target[k, 2 * j + 1] = rows[RB:]

    def fill(j, carry):
        fill_from(stack, pack, quarter_ok, pos4, j)
        return carry

    lax.fori_loop(0, NC // 2, fill, 0)

    def send_from(source, target, send_sem, recv_sem, c):
        def one(m, inner):
            rows = pl.ds(pl.multiple_of(m * 16, 16), 16)
            for k in range(2):
                pltpu.make_async_remote_copy(
                    src_ref=source.at[k, c, rows],
                    dst_ref=target.at[k, c, rows],
                    send_sem=send_sem.at[k, c],
                    recv_sem=recv_sem.at[k, c],
                    device_id=(rep, partner(c, m, 1)),
                    device_id_type=MESH,
                ).start()
            return inner

        lax.fori_loop(jnp.where(c == 0, 1, 0), NM, one, 0)

    def send_chunk(c, carry):
        send_from(pack, land, a2a_s, a2a_r, c)
        return carry

    def send_extra(c, carry):
        send_from(epack, eland, ea2a_s, ea2a_r, c)
        return carry

    def ring(src, dst, send_sem, recv_sem, peer):
        return pltpu.make_async_remote_copy(
            src_ref=src, dst_ref=dst, send_sem=send_sem, recv_sem=recv_sem,
            device_id=(peer, ep), device_id_type=MESH,
        )

    def raw_one(k):
        own = estack.at[k, pl.ds(0, 128)]
        return (
            ring(own, estack.at[k, pl.ds(128, 128)], raw1_s.at[k, 0], raw1_r.at[k, 0], pair),
            ring(own, estack.at[k, pl.ds(256, 128)], raw1_s.at[k, 1], raw1_r.at[k, 1], other),
        )

    def raw_two(k):
        return (
            ring(
                estack.at[k, pl.ds(128, 64)], estack.at[k, pl.ds(384, 64)],
                raw2_s.at[k, 0], raw2_r.at[k, 0], other,
            ),
            ring(
                estack.at[k, pl.ds(320, 64)], estack.at[k, pl.ds(448, 64)],
                raw2_s.at[k, 1], raw2_r.at[k, 1], pair,
            ),
        )

    pos_copies = [
        ring(pos_own, pos_recv.at[j], pos_s.at[j], pos_r.at[j], peer) for j, peer in enumerate((pair, other, across))
    ]
    weight_copies = [
        ring(wnat.at[k, :, theirs], wpair.at[pl.ds(k * HID, HID)], wx_s.at[k], wx_r.at[k], pair) for k in range(2)
    ]

    pl.semaphore_wait(barrier, 66)
    for copy in pos_copies:
        copy.start()
    for k in range(2):
        for copy in raw_one(k):
            copy.start()
    for k in range(2):
        pltpu.make_async_copy(pack.at[k, 0, pl.ds(0, 16)], land.at[k, 0, pl.ds(0, 16)], a2a_r.at[k, 0]).start()
    lax.fori_loop(0, 2, send_chunk, 0)
    for k in range(2):
        for one, two in zip(raw_one(k), raw_two(k)):
            one.wait_recv()
            two.start()
    for load in loads:
        load.wait()

    def pack_extra():
        for k in range(2):
            for copy in raw_two(k):
                copy.wait_recv()
        for copy in pos_copies:
            copy.wait_recv()
        places = jnp.concatenate([pos_own[:1, :]] + [pos_recv[j, :1, :] for j in range(3)], axis=1).astype(jnp.int32)

        def one(j, carry):
            fill_from(estack, epack, block_ok, places, j)
            return carry

        lax.fori_loop(0, NC // 2, one, 0)
        for k in range(2):
            pltpu.make_async_copy(
                epack.at[k, 0, pl.ds(0, 16)], eland.at[k, 0, pl.ds(0, 16)], ea2a_r.at[k, 0]
            ).start()

    def turn_weights():
        def turn(j, carry):
            cols = pl.ds(pl.multiple_of(j * 512, 512), 512)
            for k in range(3):
                wtr[k, cols, :] = wnat[k, :, cols].T
            return carry

        lax.fori_loop(0, 8, turn, 0)

    def gather_one(k, c):
        own = land.at[k, c, pl.ds(0, RB)]
        return (
            ring(own, land.at[k, c, pl.ds(RB, RB)], ag1_s.at[k, 0, c], ag1_r.at[k, 0, c], pair),
            ring(own, land.at[k, c, pl.ds(2 * RB, RB)], ag1_s.at[k, 1, c], ag1_r.at[k, 1, c], other),
        )

    def gather_two(k, c):
        return (
            ring(
                land.at[k, c, pl.ds(RB, HR)], land.at[k, c, pl.ds(3 * RB, HR)],
                ag2_s.at[k, 0, c], ag2_r.at[k, 0, c], other,
            ),
            ring(
                land.at[k, c, pl.ds(2 * RB + HR, HR)], land.at[k, c, pl.ds(3 * RB + HR, HR)],
                ag2_s.at[k, 1, c], ag2_r.at[k, 1, c], pair,
            ),
        )

    def pre_copy(c):
        return ring(pre_own.at[c], pre_pair.at[c], pre_s.at[c], pre_r.at[c], pair)

    def scatter_one(c):
        return ring(part.at[c % SLOTS, pl.ds(2 * RB, 2 * RB)], first.at[c], rs1_s.at[c], rs1_r.at[c], other)

    def scatter_two(c):
        return ring(part.at[c % SLOTS, pl.ds(RB, RB)], second.at[c], rs2_s.at[c], rs2_r.at[c], pair)

    def gate_copies(c):
        return [
            ring(gpart.at[c], grecv.at[j, c], gt_s.at[j, c], gt_r.at[j, c], peer)
            for j, peer in enumerate((pair, other, across))
        ]

    def step_gather_one(c):
        for k in range(2):
            whole = land.at[k, c, pl.ds(0, RB)]
            pltpu.make_async_copy(whole, whole, a2a_r.at[k, c]).wait()
            for copy in gather_one(k, c):
                copy.start()

    def step_gather_two(c):
        for k in range(2):
            for one, two in zip(gather_one(k, c), gather_two(k, c)):
                one.wait_recv()
                two.start()

    def step_compute(c):
        for k in range(2):
            for copy in gather_two(k, c):
                copy.wait_recv()
                copy.wait_send()
            for copy in gather_one(k, c):
                copy.wait_send()
        for k in range(2):
            arrived = eland.at[k, c]
            pltpu.make_async_copy(arrived, arrived, ea2a_r.at[k, c]).wait()
            land[k, c] = jnp.dot(perm[0], land[k, c], preferred_element_type=F32).astype(BF16)
            eland[k, c] = jnp.dot(eperm[...], eland[k, c], preferred_element_type=F32).astype(BF16)

        def project(k, w):
            total = jnp.dot(eland[k, c], wtr[w, MAIN:, :], preferred_element_type=F32)
            for q in range(NQ):
                rows = land[k, c, q * 64 : (q + 1) * 64, :]
                total = total + jnp.dot(rows, wtr[w, q * MW : (q + 1) * MW, :], preferred_element_type=F32)
            return total

        gate_pre, up_pre, weighted = project(0, 0), project(0, 1), project(1, 2)
        logistic = jax.nn.sigmoid(gate_pre)
        activated = gate_pre * logistic
        hidden = (activated * up_pre).astype(BF16)
        pre_grad = (weighted * up_pre * logistic * (1.0 + gate_pre * (1.0 - logistic))).astype(BF16)
        up_grad = (weighted * activated).astype(BF16)
        gate_sum = jnp.sum(hidden.astype(F32) * weighted, axis=1, keepdims=True)
        gate_sum = jnp.broadcast_to(jnp.concatenate([gate_sum, gate_sum], axis=0), (128, 128))
        gpart[c] = gate_sum.T[:1, :]
        rows = pl.ds(pl.multiple_of(c * 64, 64), 64)
        acts[0, rows, :] = pre_grad
        acts[1, rows, :] = up_grad
        acts[2, rows, :] = hidden
        pre_own[c] = jnp.concatenate([pre_grad, up_grad], axis=1)
        pre_copy(c).start()
        for copy in gate_copies(c):
            copy.start()

    def step_scatter_one(c):
        rows = pl.ds(pl.multiple_of(c * 64, 64), 64)
        total = jnp.dot(acts[0, rows, :], wnat[0, :, mine], preferred_element_type=F32)
        total = total + jnp.dot(acts[1, rows, :], wnat[1, :, mine], preferred_element_type=F32)
        pl.when(c == 0)(lambda: [copy.wait_recv() for copy in weight_copies] and None)
        pre_copy(c).wait()
        swapped = jnp.concatenate([pre_pair[c, b * 16 : (b + 1) * 16, :] for b in (1, 0, 3, 2)], axis=0)
        total = total + jnp.dot(swapped, wpair[...], preferred_element_type=F32)
        total = total.astype(BF16)
        stacked = jnp.concatenate([total[:, q * HW : (q + 1) * HW] for q in range(NQ)], axis=0)
        part[c % SLOTS] = jnp.dot(perm[1], stacked, preferred_element_type=F32).astype(BF16)
        scatter_one(c).start()

    def step_scatter_two(c):
        p = c % SLOTS
        scatter_one(c).wait_recv()
        total = part[p, RB : 2 * RB, :].astype(F32) + first[c, RB:, :].astype(F32)
        part[p, RB : 2 * RB, :] = total.astype(BF16)
        scatter_two(c).start()

    gr = lax.broadcasted_iota(jnp.int32, (RB, 128), 0)
    gl = lax.broadcasted_iota(jnp.int32, (RB, 128), 1)
    slot_lane = (gr >> 4) * CAP + (gr & 3)

    def ret_copy(c, m):
        rows = pl.ds(pl.multiple_of(m * 16, 16), 16)
        return pltpu.make_async_remote_copy(
            src_ref=ret.at[c, rows],
            dst_ref=back.at[c, rows],
            send_sem=ret_s.at[c],
            recv_sem=ret_r.at[c],
            device_id=(rep, partner(c, m, -1)),
            device_id_type=MESH,
        )

    def step_return(c):
        p = c % SLOTS
        scatter_two(c).wait()
        scatter_one(c).wait_send()
        for copy in gate_copies(c):
            copy.wait()
        total = part[p, :RB, :].astype(F32) + first[c, :RB, :].astype(F32)
        ret[c, :, pl.ds(pl.multiple_of(half * HW, HW), HW)] = total.astype(BF16)
        ret[c, :, pl.ds(pl.multiple_of((1 - half) * HW, HW), HW)] = second[c]
        gate = jnp.where(gl == slot_lane, gpart[c], 0.0)
        gate = gate + jnp.where(gl == slot_lane + NM * CAP, grecv[0, c], 0.0)
        gate = gate + jnp.where(gl == slot_lane + 2 * NM * CAP, grecv[1, c], 0.0)
        gate = gate + jnp.where(gl == slot_lane + 3 * NM * CAP, grecv[2, c], 0.0)
        gate = jnp.sum(gate, axis=1, keepdims=True)
        ret[c, :, QW:] = jnp.broadcast_to(gate, (RB, 128)).astype(BF16)

        @pl.when(c == 0)
        def _():
            pltpu.make_async_copy(ret.at[0, pl.ds(0, 16)], back.at[0, pl.ds(0, 16)], ret_r.at[0]).start()

        def one(m, carry):
            ret_copy(c, m).start()
            return carry

        lax.fori_loop(jnp.where(c == 0, 1, 0), NM, one, 0)

    def grad_tile(x, cot, at, wide):
        out = pl.ds(pl.multiple_of(at, 128), wide)
        dout[0, :, out] = jnp.dot(acts_t[0], x, preferred_element_type=F32).astype(BF16)
        dout[1, :, out] = jnp.dot(acts_t[1], x, preferred_element_type=F32).astype(BF16)
        dout[2, :, out] = jnp.dot(acts_t[2], cot, preferred_element_type=F32).astype(BF16)

    def weight_grads(q, carry):
        rows = pl.ds(pl.multiple_of(q * 64, 64), 64)
        for at in range(0, MW, 256):
            wide = min(256, MW - at)
            x, cot = (land[k, :, rows, at : at + wide].reshape(NC * 64, wide) for k in range(2))
            grad_tile(x, cot, q * MW + at, wide)
        return carry

    def weight_grads_extra():
        for at in range(0, EW, 256):
            x, cot = (eland[k, :, :, at : at + 256].reshape(NC * 64, 256) for k in range(2))
            grad_tile(x, cot, MAIN + at, 256)

    def turn_acts():
        for k in range(3):
            acts_t[k] = acts[k].T

    def step(t, carry):
        pl.when(t < NC)(lambda: step_gather_one(t))
        pl.when((t >= 1) & (t < NC + 1))(lambda: step_gather_two(t - 1))
        pl.when(t == 1)(pack_extra)
        main_first, main_last = pick(t, (2, 6, 9, 12)), pick(t, (6, 9, 12, 16))
        extra_first, extra_last = pick(t, (0, 0, 4, 9)), pick(t, (0, 4, 9, 16))
        lax.fori_loop(extra_first, extra_last, send_extra, 0)
        lax.fori_loop(main_first, main_last, send_chunk, 0)
        pl.when(t == 1)(turn_weights)
        pl.when(t == 1)(lambda: [copy.start() for copy in weight_copies] and None)
        pl.when((t >= 2) & (t < NC + 2))(lambda: step_compute(t - 2))
        pl.when((t >= 3) & (t < NC + 3))(lambda: step_scatter_one(t - 3))
        pl.when((t >= 4) & (t < NC + 4))(lambda: step_scatter_two(t - 4))
        pl.when((t >= 5) & (t < NC + 5))(lambda: step_return(t - 5))
        pl.when(t == NC + 1)(turn_acts)
        u = t - NC
        lax.fori_loop(pick(u, (0, 0, 1, 2, 3)), pick(u, (0, 1, 2, 3, 4)), weight_grads, 0)
        pl.when(t == NC + 4)(weight_grads_extra)
        return carry

    lax.fori_loop(0, NC + 5, step, 0)

    stores = [
        pltpu.make_async_copy(dout.at[k], dst.at[0], o_sem.at[k])
        for k, dst in enumerate((dg_ref, du_ref, dd_ref))
    ]
    for store in stores:
        store.start()
    skip = pl.ds(16, RB - 16)
    for c in range(NC):
        pltpu.make_async_copy(back.at[c], back.at[c], ret_r.at[c]).wait()
        rows = skip if c == 0 else pl.ds(0, RB)
        for k in range(2):
            pltpu.make_async_copy(pack.at[k, c, rows], pack.at[k, c, rows], a2a_s.at[k, c]).wait()
            pltpu.make_async_copy(epack.at[k, c, rows], epack.at[k, c, rows], ea2a_s.at[k, c]).wait()
        pltpu.make_async_copy(ret.at[c, rows], ret.at[c, rows], ret_s.at[c]).wait()
    for k in range(2):
        for copy in raw_one(k) + raw_two(k):
            copy.wait_send()
    for copy in pos_copies + weight_copies:
        copy.wait_send()
    for store in stores:
        store.wait()


def finish(
    back_hbm, ids_ref, g_ref, dg_ref, du_ref, dd_ref,
    tgrad_ref, ggrad_ref, og_ref, ou_ref, od_ref,
    back, grads, b_sem, in_sem, out_sem,
):
    ep = lax.axis_index("ep")
    load = pltpu.make_async_copy(back_hbm, back, b_sem)
    load.start()
    fetches = [
        pltpu.make_async_copy(src.at[0], grads.at[k], in_sem.at[k]) for k, src in enumerate((dg_ref, du_ref, dd_ref))
    ]
    stores = [
        pltpu.make_async_copy(grads.at[k], dst.at[0], out_sem.at[k]) for k, dst in enumerate((og_ref, ou_ref, od_ref))
    ]
    for fetch in fetches:
        fetch.start()
    pos = positions(ids_ref, ep // 16, (ep // 2) % 8, ep % 2)
    pos_col = jnp.broadcast_to(pos.astype(F32), (128, 128)).T[:, :1].astype(jnp.int32)
    mr = lax.broadcasted_iota(jnp.int32, (128, NC * RB), 1)
    hit = (mr >> 4) * CAP + (mr & 3) == pos_col
    load.wait()
    for fetch, store in zip(fetches, stores):
        fetch.wait()
        store.start()
    for q in range(NQ):
        take = jnp.where(hit & (((mr >> 2) & 3) == q), 1.0, 0.0).astype(BF16)
        rows = back[:, :, :QW].reshape(NC * RB, QW)
        found = jnp.dot(take, rows, preferred_element_type=F32).astype(BF16)
        for h in range(2):
            at = h * 2048 + q * HW
            tgrad_ref[:, at : at + HW] = found[:, h * HW : (h + 1) * HW]
        if q == 0:
            gate = jnp.dot(take, back[:, :, QW:].reshape(NC * RB, 128), preferred_element_type=F32)
            ggrad_ref[...] = (gate.T[:1, :] / g_ref[...].astype(F32)).astype(BF16)
    for store in stores:
        store.wait()


def shards(tokens, cotangent, expert_ids, gates, gate_weight, up_weight, down_weight):
    rows, width = tokens.shape
    vmem, hbm = pl.BlockSpec(memory_space=pltpu.VMEM), pl.BlockSpec(memory_space=pl.ANY)
    dma = pltpu.SemaphoreType.DMA
    ids, gates = expert_ids.reshape(1, rows), gates.reshape(1, rows)
    weight_shape = jax.ShapeDtypeStruct((1, HID, width), BF16)
    back, *grads = pl.pallas_call(
        kernel,
        out_shape=(jax.ShapeDtypeStruct((NC, RB, BW), BF16),) + (weight_shape,) * 3,
        in_specs=[vmem] * 4 + [hbm] * 3,
        out_specs=(hbm,) * 4,
        scratch_shapes=[
            pltpu.VMEM((2, NC, 4 * RB, MW), BF16),
            pltpu.VMEM((2, NC, RB, MW), BF16),
            pltpu.VMEM((2, NQ * 128, MW), BF16),
            pltpu.VMEM((2, NC, RB, EW), BF16),
            pltpu.VMEM((2, NC, RB, EW), BF16),
            pltpu.VMEM((2, 4 * 128, EW), BF16),
            pltpu.VMEM((8, 128), F32),
            pltpu.VMEM((3, 8, 128), F32),
            pltpu.VMEM((2, 256, 256), BF16),
            pltpu.VMEM((64, 64), BF16),
            pltpu.VMEM((3, HID, width), BF16),
            pltpu.VMEM((3, width, HID), BF16),
            pltpu.VMEM((2 * HID, width // 2), BF16),
            pltpu.VMEM((NC, 64, 2 * HID), BF16),
            pltpu.VMEM((NC, 64, 2 * HID), BF16),
            pltpu.VMEM((SLOTS, 4 * RB, HW), BF16),
            pltpu.VMEM((NC, 2 * RB, HW), BF16),
            pltpu.VMEM((NC, RB, HW), BF16),
            pltpu.VMEM((NC, 1, 128), F32),
            pltpu.VMEM((3, NC, 1, 128), F32),
            pltpu.VMEM((NC, RB, BW), BF16),
            pltpu.VMEM((3, NC * 64, HID), BF16),
            pltpu.VMEM((3, HID, NC * 64), BF16),
            pltpu.VMEM((3, HID, width), BF16),
            dma((2, NC)), dma((2, NC)), dma((2, NC)), dma((2, NC)),
            dma((2, 2)), dma((2, 2)), dma((2, 2)), dma((2, 2)), dma((3,)), dma((3,)),
            dma((2, 2, NC)), dma((2, 2, NC)), dma((2, 2, NC)), dma((2, 2, NC)),
            dma((NC,)), dma((NC,)), dma((NC,)), dma((NC,)), dma((NC,)), dma((NC,)), dma((2,)), dma((2,)),
            dma((3, NC)), dma((3, NC)),
            dma((NC,)), dma((NC,)),
            dma((3,)), dma((3,)),
        ],
        compiler_params=pltpu.CompilerParams(
            collective_id=0, has_side_effects=True, vmem_limit_bytes=62 * 1024 * 1024
        ),
    )(
        tokens,
        cotangent,
        ids,
        gates,
        jnp.transpose(gate_weight, (0, 2, 1)),
        jnp.transpose(up_weight, (0, 2, 1)),
        down_weight,
    )
    token_grad, gates_grad, gate_grad, upper_grad, down_grad = pl.pallas_call(
        finish,
        out_shape=(
            jax.ShapeDtypeStruct((rows, width), BF16),
            jax.ShapeDtypeStruct((1, rows), BF16),
        ) + (weight_shape,) * 3,
        in_specs=[hbm, vmem, vmem] + [hbm] * 3,
        out_specs=(vmem, vmem, hbm, hbm, hbm),
        scratch_shapes=[
            pltpu.VMEM((NC, RB, BW), BF16), pltpu.VMEM((3, HID, width), BF16), dma, dma((3,)), dma((3,)),
        ],
        compiler_params=pltpu.CompilerParams(vmem_limit_bytes=62 * 1024 * 1024),
    )(back, ids, gates, *grads)
    return (
        token_grad,
        gates_grad.reshape(rows, 1),
        jnp.transpose(gate_grad, (0, 2, 1)),
        jnp.transpose(upper_grad, (0, 2, 1)),
        down_grad,
    )


def solution(mesh):
    in_specs = (
        P(("rep", "ep"), None),
        P(("rep", "ep"), None),
        P(("rep", "ep"), None),
        P(("rep", "ep"), None),
        P("ep", None, "rep"),
        P("ep", None, "rep"),
        P("ep", "rep", None),
    )
    out_specs = (
        P(("rep", "ep"), None),
        P(("rep", "ep"), None),
        P("ep", None, "rep"),
        P("ep", None, "rep"),
        P("ep", "rep", None),
    )
    return jax.shard_map(shards, mesh=mesh, in_specs=in_specs, out_specs=out_specs, check_vma=False)
```

```python
import jax
import jax.numpy as jnp
from jax import lax
from jax.experimental import pallas as pl
from jax.experimental.pallas import tpu as pltpu
from jax.sharding import PartitionSpec as P

MESH = pl.DeviceIdType.MESH
F32, BF16 = jnp.float32, jnp.bfloat16

DZ = (0, 7, 2, 5, 3, 4, 6, 1)
NC = 16
NM = 4
CAP = 4
NQ = 4
RB = NM * NQ * CAP
HR = RB // 2
QW = 1024
HW = 512
EW = 512
MW = QW - EW // NQ
MAIN = NQ * MW
BW = QW + 128
HID = 192
SLOTS = 3
ROWS = NC * NM * CAP


def pick(index, table):
    return sum(jnp.where(index == k, v, 0) for k, v in enumerate(table) if v)


def positions(ids_ref, my_y, my_z, my_c):
    ids = ids_ref[...].astype(F32)
    by_lane = jnp.broadcast_to(ids, (128, 128))
    by_row = by_lane.T
    a = lax.broadcasted_iota(jnp.int32, (128, 128), 0)
    b = lax.broadcasted_iota(jnp.int32, (128, 128), 1)
    same = jnp.where(by_lane == by_row, 1, 0)
    rank = jnp.sum(jnp.where(a < b, same, 0), axis=0, keepdims=True)
    expert = ids_ref[...]
    dy = ((expert >> 4) - my_y) & 3
    dz = (((expert >> 1) & 7) - my_z) & 7
    dc = (expert - my_c) & 1
    at_z = sum(jnp.where(dz == d, k, 0) for k, d in enumerate(DZ) if k)
    return ((at_z * 2 + dc) * NM + dy) * CAP + rank


def kernel(
    tok_ref, cot_ref, ids_ref, g_ref, wg_ref, wu_ref, wd_ref,
    back, dg_ref, du_ref, dd_ref,
    land, pack, stack, eland, epack, estack, pos_own, pos_recv, perm, eperm, wnat, wtr, wpair, pre_own, pre_pair, part, first, second, gpart, grecv, ret, acts, acts_t, dout,
    a2a_s, a2a_r, ea2a_s, ea2a_r, raw1_s, raw1_r, raw2_s, raw2_r, pos_s, pos_r, ag1_s, ag1_r, ag2_s, ag2_r, rs1_s, rs1_r, rs2_s, rs2_r, pre_s, pre_r, wx_s, wx_r, gt_s, gt_r, ret_s, ret_r, w_sem, o_sem,
):
    rep, ep = lax.axis_index("rep"), lax.axis_index("ep")
    my_y, my_z, my_c = ep // 16, (ep // 2) % 8, ep % 2
    side = 1 - 2 * ((rep + my_c) % 2)
    pair, other, across = (rep + side + 4) % 4, (rep - side + 4) % 4, (rep + 2) % 4
    half = ((rep + 1 - my_c) // 2) % 2
    mine, theirs = (pl.ds(pl.multiple_of(h * 2048, 2048), 2048) for h in (half, 1 - half))

    loads = [
        pltpu.make_async_copy(src.at[0], wnat.at[k], w_sem.at[k])
        for k, src in enumerate((wg_ref, wu_ref, wd_ref))
    ]
    for load in loads:
        load.start()

    barrier = pltpu.get_barrier_semaphore()

    def greet(k, carry):
        pl.semaphore_signal(barrier, inc=1, device_id=(rep, (ep + k) % 64), device_id_type=MESH)
        return carry

    lax.fori_loop(1, 64, greet, 0)
    for peer in (pair, other, across):
        pl.semaphore_signal(barrier, inc=1, device_id=(peer, ep), device_id_type=MESH)

    pos = positions(ids_ref, my_y, my_z, my_c)
    gates_row = g_ref[...].astype(F32)
    gates_col = jnp.broadcast_to(gates_row, (128, 128)).T[:, :1]
    pos_own[...] = jnp.broadcast_to(pos.astype(F32), (8, 128))
    for q in range(NQ):
        stack[0, q * 128 : (q + 1) * 128, :] = tok_ref[:, q * MW : (q + 1) * MW]
        cot = cot_ref[:, q * MW : (q + 1) * MW].astype(F32)
        stack[1, q * 128 : (q + 1) * 128, :] = (cot * gates_col).astype(BF16)
    estack[0, :128, :] = tok_ref[:, MAIN:]
    estack[1, :128, :] = (cot_ref[:, MAIN:].astype(F32) * gates_col).astype(BF16)

    pr = lax.broadcasted_iota(jnp.int32, (256, 256), 0)
    pc = lax.broadcasted_iota(jnp.int32, (256, 256), 1)
    perm[0] = jnp.where(pc == ((pr & 63) >> 2) * 16 + (pr >> 6) * 4 + (pr & 3), 1.0, 0.0).astype(BF16)
    perm[1] = jnp.where(pr == ((pc & 63) >> 2) * 16 + (pc >> 6) * 4 + (pc & 3), 1.0, 0.0).astype(BF16)

    er = lax.broadcasted_iota(jnp.int32, (64, 64), 0)
    ec = lax.broadcasted_iota(jnp.int32, (64, 64), 1)
    eperm[...] = jnp.where(ec == ((er & 15) >> 2) * 16 + (er >> 4) * 4 + (er & 3), 1.0, 0.0).astype(BF16)

    def partner(c, m, sign):
        z = (my_z + sign * pick(c // 2, DZ) + 8) % 8
        y = (my_y + sign * m + 4) % 4
        return y * 16 + z * 2 + (my_c + c) % 2

    sr = lax.broadcasted_iota(jnp.int32, (2 * RB, 512), 0)
    sc = lax.broadcasted_iota(jnp.int32, (2 * RB, 512), 1)
    slot_of_row = (sr >> 4) * CAP + (sr & 3)
    quarter = (sr >> 2) & 3
    quarter_ok = quarter == (sc >> 7)
    changed = (sr >= RB) & ((quarter == 1) | (quarter == 2))
    block_ok = jnp.where(changed, 3 - quarter, quarter) == (sc >> 7)
    pos4 = jnp.concatenate([pos] * NQ, axis=1)

    def fill_from(source, target, ok, places, j):
        onehot = jnp.where(ok & (places - j * (2 * NM * CAP) == slot_of_row), 1.0, 0.0).astype(BF16)
        for k in range(2):
            rows = jnp.dot(onehot, source[k], preferred_element_type=F32).astype(BF16)
            target[k, 2 * j] = rows[:RB]
            target[k, 2 * j + 1] = rows[RB:]

    def fill(j, carry):
        fill_from(stack, pack, quarter_ok, pos4, j)
        return carry

    fill(0, 0)

    def send_from(source, target, send_sem, recv_sem, c):
        def one(m, inner):
            rows = pl.ds(pl.multiple_of(m * 16, 16), 16)
            for k in range(2):
                pltpu.make_async_remote_copy(
                    src_ref=source.at[k, c, rows],
                    dst_ref=target.at[k, c, rows],
                    send_sem=send_sem.at[k, c],
                    recv_sem=recv_sem.at[k, c],
                    device_id=(rep, partner(c, m, 1)),
                    device_id_type=MESH,
                ).start()
            return inner

        lax.fori_loop(jnp.where(c == 0, 1, 0), NM, one, 0)

    def send_chunk(c, carry):
        send_from(pack, land, a2a_s, a2a_r, c)
        return carry

    def send_extra(c, carry):
        send_from(epack, eland, ea2a_s, ea2a_r, c)
        return carry

    def ring(src, dst, send_sem, recv_sem, peer):
        return pltpu.make_async_remote_copy(
            src_ref=src, dst_ref=dst, send_sem=send_sem, recv_sem=recv_sem,
            device_id=(peer, ep), device_id_type=MESH,
        )

    def raw_one(k):
        own = estack.at[k, pl.ds(0, 128)]
        return (
            ring(own, estack.at[k, pl.ds(128, 128)], raw1_s.at[k, 0], raw1_r.at[k, 0], pair),
            ring(own, estack.at[k, pl.ds(256, 128)], raw1_s.at[k, 1], raw1_r.at[k, 1], other),
        )

    def raw_two(k):
        return (
            ring(
                estack.at[k, pl.ds(128, 64)], estack.at[k, pl.ds(384, 64)],
                raw2_s.at[k, 0], raw2_r.at[k, 0], other,
            ),
            ring(
                estack.at[k, pl.ds(320, 64)], estack.at[k, pl.ds(448, 64)],
                raw2_s.at[k, 1], raw2_r.at[k, 1], pair,
            ),
        )

    pos_copies = [
        ring(pos_own, pos_recv.at[j], pos_s.at[j], pos_r.at[j], peer) for j, peer in enumerate((pair, other, across))
    ]
    weight_copies = [
        ring(wnat.at[k, :, theirs], wpair.at[pl.ds(k * HID, HID)], wx_s.at[k], wx_r.at[k], pair) for k in range(2)
    ]

    pl.semaphore_wait(barrier, 66)
    for copy in pos_copies:
        copy.start()
    for k in range(2):
        for copy in raw_one(k):
            copy.start()
    for k in range(2):
        pltpu.make_async_copy(pack.at[k, 0, pl.ds(0, 16)], land.at[k, 0, pl.ds(0, 16)], a2a_r.at[k, 0]).start()
    lax.fori_loop(0, 2, send_chunk, 0)
    lax.fori_loop(1, NC // 2, fill, 0)
    for k in range(2):
        for one, two in zip(raw_one(k), raw_two(k)):
            one.wait_recv()
            two.start()
    for load in loads:
        load.wait()

    def pack_extra():
        for k in range(2):
            for copy in raw_two(k):
                copy.wait_recv()
        for copy in pos_copies:
            copy.wait_recv()
        places = jnp.concatenate([pos_own[:1, :]] + [pos_recv[j, :1, :] for j in range(3)], axis=1).astype(jnp.int32)

        def one(j, carry):
            fill_from(estack, epack, block_ok, places, j)
            return carry

        lax.fori_loop(0, NC // 2, one, 0)
        for k in range(2):
            pltpu.make_async_copy(
                epack.at[k, 0, pl.ds(0, 16)], eland.at[k, 0, pl.ds(0, 16)], ea2a_r.at[k, 0]
            ).start()

    def turn_weights():
        def turn(j, carry):
            cols = pl.ds(pl.multiple_of(j * 512, 512), 512)
            for k in range(3):
                wtr[k, cols, :] = wnat[k, :, cols].T
            return carry

        lax.fori_loop(0, 8, turn, 0)

    def gather_one(k, c):
        own = land.at[k, c, pl.ds(0, RB)]
        return (
            ring(own, land.at[k, c, pl.ds(RB, RB)], ag1_s.at[k, 0, c], ag1_r.at[k, 0, c], pair),
            ring(own, land.at[k, c, pl.ds(2 * RB, RB)], ag1_s.at[k, 1, c], ag1_r.at[k, 1, c], other),
        )

    def gather_two(k, c):
        return (
            ring(
                land.at[k, c, pl.ds(RB, HR)], land.at[k, c, pl.ds(3 * RB, HR)],
                ag2_s.at[k, 0, c], ag2_r.at[k, 0, c], other,
            ),
            ring(
                land.at[k, c, pl.ds(2 * RB + HR, HR)], land.at[k, c, pl.ds(3 * RB + HR, HR)],
                ag2_s.at[k, 1, c], ag2_r.at[k, 1, c], pair,
            ),
        )

    def pre_copy(c):
        return ring(pre_own.at[c], pre_pair.at[c], pre_s.at[c], pre_r.at[c], pair)

    def scatter_one(c):
        return ring(part.at[c % SLOTS, pl.ds(2 * RB, 2 * RB)], first.at[c], rs1_s.at[c], rs1_r.at[c], other)

    def scatter_two(c):
        return ring(part.at[c % SLOTS, pl.ds(RB, RB)], second.at[c], rs2_s.at[c], rs2_r.at[c], pair)

    def gate_copies(c):
        return [
            ring(gpart.at[c], grecv.at[j, c], gt_s.at[j, c], gt_r.at[j, c], peer)
            for j, peer in enumerate((pair, other, across))
        ]

    def step_gather_one(c):
        for k in range(2):
            whole = land.at[k, c, pl.ds(0, RB)]
            pltpu.make_async_copy(whole, whole, a2a_r.at[k, c]).wait()
            for copy in gather_one(k, c):
                copy.start()

    def step_gather_two(c):
        for k in range(2):
            for one, two in zip(gather_one(k, c), gather_two(k, c)):
                one.wait_recv()
                two.start()

    def step_compute(c):
        for k in range(2):
            for copy in gather_two(k, c):
                copy.wait_recv()
                copy.wait_send()
            for copy in gather_one(k, c):
                copy.wait_send()
        for k in range(2):
            arrived = eland.at[k, c]
            pltpu.make_async_copy(arrived, arrived, ea2a_r.at[k, c]).wait()
            land[k, c] = jnp.dot(perm[0], land[k, c], preferred_element_type=F32).astype(BF16)
            eland[k, c] = jnp.dot(eperm[...], eland[k, c], preferred_element_type=F32).astype(BF16)

        def project(k, w):
            total = jnp.dot(eland[k, c], wtr[w, MAIN:, :], preferred_element_type=F32)
            for q in range(NQ):
                rows = land[k, c, q * 64 : (q + 1) * 64, :]
                total = total + jnp.dot(rows, wtr[w, q * MW : (q + 1) * MW, :], preferred_element_type=F32)
            return total

        gate_pre, up_pre, weighted = project(0, 0), project(0, 1), project(1, 2)
        logistic = jax.nn.sigmoid(gate_pre)
        activated = gate_pre * logistic
        hidden = (activated * up_pre).astype(BF16)
        pre_grad = (weighted * up_pre * logistic * (1.0 + gate_pre * (1.0 - logistic))).astype(BF16)
        up_grad = (weighted * activated).astype(BF16)
        gate_sum = jnp.sum(hidden.astype(F32) * weighted, axis=1, keepdims=True)
        gate_sum = jnp.broadcast_to(jnp.concatenate([gate_sum, gate_sum], axis=0), (128, 128))
        gpart[c] = gate_sum.T[:1, :]
        rows = pl.ds(pl.multiple_of(c * 64, 64), 64)
        acts[0, rows, :] = pre_grad
        acts[1, rows, :] = up_grad
        acts[2, rows, :] = hidden
        pre_own[c] = jnp.concatenate([pre_grad, up_grad], axis=1)
        pre_copy(c).start()
        for copy in gate_copies(c):
            copy.start()

    def step_scatter_one(c):
        rows = pl.ds(pl.multiple_of(c * 64, 64), 64)
        total = jnp.dot(acts[0, rows, :], wnat[0, :, mine], preferred_element_type=F32)
        total = total + jnp.dot(acts[1, rows, :], wnat[1, :, mine], preferred_element_type=F32)
        pl.when(c == 0)(lambda: [copy.wait_recv() for copy in weight_copies] and None)
        pre_copy(c).wait()
        swapped = jnp.concatenate([pre_pair[c, b * 16 : (b + 1) * 16, :] for b in (1, 0, 3, 2)], axis=0)
        total = total + jnp.dot(swapped, wpair[...], preferred_element_type=F32)
        total = total.astype(BF16)
        stacked = jnp.concatenate([total[:, q * HW : (q + 1) * HW] for q in range(NQ)], axis=0)
        part[c % SLOTS] = jnp.dot(perm[1], stacked, preferred_element_type=F32).astype(BF16)
        scatter_one(c).start()

    def step_scatter_two(c):
        p = c % SLOTS
        scatter_one(c).wait_recv()
        total = part[p, RB : 2 * RB, :].astype(F32) + first[c, RB:, :].astype(F32)
        part[p, RB : 2 * RB, :] = total.astype(BF16)
        scatter_two(c).start()

    gr = lax.broadcasted_iota(jnp.int32, (RB, 128), 0)
    gl = lax.broadcasted_iota(jnp.int32, (RB, 128), 1)
    slot_lane = (gr >> 4) * CAP + (gr & 3)

    def ret_copy(c, m):
        rows = pl.ds(pl.multiple_of(m * 16, 16), 16)
        return pltpu.make_async_remote_copy(
            src_ref=ret.at[c, rows],
            dst_ref=back.at[c, rows],
            send_sem=ret_s.at[c],
            recv_sem=ret_r.at[c],
            device_id=(rep, partner(c, m, -1)),
            device_id_type=MESH,
        )

    def step_return(c):
        p = c % SLOTS
        scatter_two(c).wait()
        scatter_one(c).wait_send()
        for copy in gate_copies(c):
            copy.wait()
        total = part[p, :RB, :].astype(F32) + first[c, :RB, :].astype(F32)
        ret[c, :, pl.ds(pl.multiple_of(half * HW, HW), HW)] = total.astype(BF16)
        ret[c, :, pl.ds(pl.multiple_of((1 - half) * HW, HW), HW)] = second[c]
        gate = jnp.where(gl == slot_lane, gpart[c], 0.0)
        gate = gate + jnp.where(gl == slot_lane + NM * CAP, grecv[0, c], 0.0)
        gate = gate + jnp.where(gl == slot_lane + 2 * NM * CAP, grecv[1, c], 0.0)
        gate = gate + jnp.where(gl == slot_lane + 3 * NM * CAP, grecv[2, c], 0.0)
        gate = jnp.sum(gate, axis=1, keepdims=True)
        ret[c, :, QW:] = jnp.broadcast_to(gate, (RB, 128)).astype(BF16)

        @pl.when(c == 0)
        def _():
            pltpu.make_async_copy(ret.at[0, pl.ds(0, 16)], back.at[0, pl.ds(0, 16)], ret_r.at[0]).start()

        def one(m, carry):
            ret_copy(c, m).start()
            return carry

        lax.fori_loop(jnp.where(c == 0, 1, 0), NM, one, 0)

    def grad_tile(x, cot, at, wide):
        out = pl.ds(pl.multiple_of(at, 128), wide)
        dout[0, :, out] = jnp.dot(acts_t[0], x, preferred_element_type=F32).astype(BF16)
        dout[1, :, out] = jnp.dot(acts_t[1], x, preferred_element_type=F32).astype(BF16)
        dout[2, :, out] = jnp.dot(acts_t[2], cot, preferred_element_type=F32).astype(BF16)

    def weight_grads(q, carry):
        rows = pl.ds(pl.multiple_of(q * 64, 64), 64)
        for at in range(0, MW, 256):
            wide = min(256, MW - at)
            x, cot = (land[k, :, rows, at : at + wide].reshape(NC * 64, wide) for k in range(2))
            grad_tile(x, cot, q * MW + at, wide)
        return carry

    def weight_grads_extra():
        for at in range(0, EW, 256):
            x, cot = (eland[k, :, :, at : at + 256].reshape(NC * 64, 256) for k in range(2))
            grad_tile(x, cot, MAIN + at, 256)

    def turn_acts():
        for k in range(3):
            acts_t[k] = acts[k].T

    def step(t, carry):
        pl.when(t < NC)(lambda: step_gather_one(t))
        pl.when((t >= 1) & (t < NC + 1))(lambda: step_gather_two(t - 1))
        pl.when(t == 1)(pack_extra)
        main_first, main_last = pick(t, (2, 6, 9, 12)), pick(t, (6, 9, 12, 16))
        extra_first, extra_last = pick(t, (0, 0, 4, 9)), pick(t, (0, 4, 9, 16))
        lax.fori_loop(extra_first, extra_last, send_extra, 0)
        lax.fori_loop(main_first, main_last, send_chunk, 0)
        pl.when(t == 1)(turn_weights)
        pl.when(t == 1)(lambda: [copy.start() for copy in weight_copies] and None)
        pl.when((t >= 2) & (t < NC + 2))(lambda: step_compute(t - 2))
        pl.when((t >= 3) & (t < NC + 3))(lambda: step_scatter_one(t - 3))
        pl.when((t >= 4) & (t < NC + 4))(lambda: step_scatter_two(t - 4))
        pl.when((t >= 5) & (t < NC + 5))(lambda: step_return(t - 5))
        pl.when(t == NC + 1)(turn_acts)
        u = t - NC
        lax.fori_loop(pick(u, (0, 0, 1, 2, 3)), pick(u, (0, 1, 2, 3, 4)), weight_grads, 0)
        pl.when(t == NC + 4)(weight_grads_extra)
        return carry

    lax.fori_loop(0, NC + 5, step, 0)

    stores = [
        pltpu.make_async_copy(dout.at[k], dst.at[0], o_sem.at[k])
        for k, dst in enumerate((dg_ref, du_ref, dd_ref))
    ]
    for store in stores:
        store.start()
    skip = pl.ds(16, RB - 16)
    for c in range(NC):
        pltpu.make_async_copy(back.at[c], back.at[c], ret_r.at[c]).wait()
        rows = skip if c == 0 else pl.ds(0, RB)
        for k in range(2):
            pltpu.make_async_copy(pack.at[k, c, rows], pack.at[k, c, rows], a2a_s.at[k, c]).wait()
            pltpu.make_async_copy(epack.at[k, c, rows], epack.at[k, c, rows], ea2a_s.at[k, c]).wait()
        pltpu.make_async_copy(ret.at[c, rows], ret.at[c, rows], ret_s.at[c]).wait()
    for k in range(2):
        for copy in raw_one(k) + raw_two(k):
            copy.wait_send()
    for copy in pos_copies + weight_copies:
        copy.wait_send()
    for store in stores:
        store.wait()


def finish(
    back_hbm, ids_ref, g_ref, dg_ref, du_ref, dd_ref,
    tgrad_ref, ggrad_ref, og_ref, ou_ref, od_ref,
    back, grads, b_sem, in_sem, out_sem,
):
    ep = lax.axis_index("ep")
    load = pltpu.make_async_copy(back_hbm, back, b_sem)
    load.start()
    fetches = [
        pltpu.make_async_copy(src.at[0], grads.at[k], in_sem.at[k]) for k, src in enumerate((dg_ref, du_ref, dd_ref))
    ]
    stores = [
        pltpu.make_async_copy(grads.at[k], dst.at[0], out_sem.at[k]) for k, dst in enumerate((og_ref, ou_ref, od_ref))
    ]
    for fetch in fetches:
        fetch.start()
    pos = positions(ids_ref, ep // 16, (ep // 2) % 8, ep % 2)
    pos_col = jnp.broadcast_to(pos.astype(F32), (128, 128)).T[:, :1].astype(jnp.int32)
    mr = lax.broadcasted_iota(jnp.int32, (128, NC * RB), 1)
    hit = (mr >> 4) * CAP + (mr & 3) == pos_col
    load.wait()
    for fetch, store in zip(fetches, stores):
        fetch.wait()
        store.start()
    for q in range(NQ):
        take = jnp.where(hit & (((mr >> 2) & 3) == q), 1.0, 0.0).astype(BF16)
        rows = back[:, :, :QW].reshape(NC * RB, QW)
        found = jnp.dot(take, rows, preferred_element_type=F32).astype(BF16)
        for h in range(2):
            at = h * 2048 + q * HW
            tgrad_ref[:, at : at + HW] = found[:, h * HW : (h + 1) * HW]
        if q == 0:
            gate = jnp.dot(take, back[:, :, QW:].reshape(NC * RB, 128), preferred_element_type=F32)
            ggrad_ref[...] = (gate.T[:1, :] / g_ref[...].astype(F32)).astype(BF16)
    for store in stores:
        store.wait()


def shards(tokens, cotangent, expert_ids, gates, gate_weight, up_weight, down_weight):
    rows, width = tokens.shape
    vmem, hbm = pl.BlockSpec(memory_space=pltpu.VMEM), pl.BlockSpec(memory_space=pl.ANY)
    dma = pltpu.SemaphoreType.DMA
    ids, gates = expert_ids.reshape(1, rows), gates.reshape(1, rows)
    weight_shape = jax.ShapeDtypeStruct((1, HID, width), BF16)
    back, *grads = pl.pallas_call(
        kernel,
        out_shape=(jax.ShapeDtypeStruct((NC, RB, BW), BF16),) + (weight_shape,) * 3,
        in_specs=[vmem] * 4 + [hbm] * 3,
        out_specs=(hbm,) * 4,
        scratch_shapes=[
            pltpu.VMEM((2, NC, 4 * RB, MW), BF16),
            pltpu.VMEM((2, NC, RB, MW), BF16),
            pltpu.VMEM((2, NQ * 128, MW), BF16),
            pltpu.VMEM((2, NC, RB, EW), BF16),
            pltpu.VMEM((2, NC, RB, EW), BF16),
            pltpu.VMEM((2, 4 * 128, EW), BF16),
            pltpu.VMEM((8, 128), F32),
            pltpu.VMEM((3, 8, 128), F32),
            pltpu.VMEM((2, 256, 256), BF16),
            pltpu.VMEM((64, 64), BF16),
            pltpu.VMEM((3, HID, width), BF16),
            pltpu.VMEM((3, width, HID), BF16),
            pltpu.VMEM((2 * HID, width // 2), BF16),
            pltpu.VMEM((NC, 64, 2 * HID), BF16),
            pltpu.VMEM((NC, 64, 2 * HID), BF16),
            pltpu.VMEM((SLOTS, 4 * RB, HW), BF16),
            pltpu.VMEM((NC, 2 * RB, HW), BF16),
            pltpu.VMEM((NC, RB, HW), BF16),
            pltpu.VMEM((NC, 1, 128), F32),
            pltpu.VMEM((3, NC, 1, 128), F32),
            pltpu.VMEM((NC, RB, BW), BF16),
            pltpu.VMEM((3, NC * 64, HID), BF16),
            pltpu.VMEM((3, HID, NC * 64), BF16),
            pltpu.VMEM((3, HID, width), BF16),
            dma((2, NC)), dma((2, NC)), dma((2, NC)), dma((2, NC)),
            dma((2, 2)), dma((2, 2)), dma((2, 2)), dma((2, 2)), dma((3,)), dma((3,)),
            dma((2, 2, NC)), dma((2, 2, NC)), dma((2, 2, NC)), dma((2, 2, NC)),
            dma((NC,)), dma((NC,)), dma((NC,)), dma((NC,)), dma((NC,)), dma((NC,)), dma((2,)), dma((2,)),
            dma((3, NC)), dma((3, NC)),
            dma((NC,)), dma((NC,)),
            dma((3,)), dma((3,)),
        ],
        compiler_params=pltpu.CompilerParams(
            collective_id=0, has_side_effects=True, vmem_limit_bytes=62 * 1024 * 1024
        ),
    )(
        tokens,
        cotangent,
        ids,
        gates,
        jnp.transpose(gate_weight, (0, 2, 1)),
        jnp.transpose(up_weight, (0, 2, 1)),
        down_weight,
    )
    token_grad, gates_grad, gate_grad, upper_grad, down_grad = pl.pallas_call(
        finish,
        out_shape=(
            jax.ShapeDtypeStruct((rows, width), BF16),
            jax.ShapeDtypeStruct((1, rows), BF16),
        ) + (weight_shape,) * 3,
        in_specs=[hbm, vmem, vmem] + [hbm] * 3,
        out_specs=(vmem, vmem, hbm, hbm, hbm),
        scratch_shapes=[
            pltpu.VMEM((NC, RB, BW), BF16), pltpu.VMEM((3, HID, width), BF16), dma, dma((3,)), dma((3,)),
        ],
        compiler_params=pltpu.CompilerParams(vmem_limit_bytes=62 * 1024 * 1024),
    )(back, ids, gates, *grads)
    return (
        token_grad,
        gates_grad.reshape(rows, 1),
        jnp.transpose(gate_grad, (0, 2, 1)),
        jnp.transpose(upper_grad, (0, 2, 1)),
        down_grad,
    )


def solution(mesh):
    in_specs = (
        P(("rep", "ep"), None),
        P(("rep", "ep"), None),
        P(("rep", "ep"), None),
        P(("rep", "ep"), None),
        P("ep", None, "rep"),
        P("ep", None, "rep"),
        P("ep", "rep", None),
    )
    out_specs = (
        P(("rep", "ep"), None),
        P(("rep", "ep"), None),
        P("ep", None, "rep"),
        P("ep", None, "rep"),
        P("ep", "rep", None),
    )
    return jax.shard_map(shards, mesh=mesh, in_specs=in_specs, out_specs=out_specs, check_vma=False)
```
